32 devices in a mesh: strip: 4 (over y, x), req: 8 (over z, core).
Axes of the slice: x: 2, y: 2, z: 4, core: 2. Of those that a mesh axis runs over, the one named last changes fastest.
Arguments:
- hidden_states: bfloat16 [2, 16, 16, 2, 14, 640], P(None, 'req', 'strip'), may hold values from -20 to 20
- gate: int32 [16], P('req'), may hold values from 0 to 1, as said below
- context_slot: int32 [16], replicated, may hold values from 0 to 15, as said below
- context_pages: bfloat16 [2, 16, 77, 640], P(None, 'req'), may hold values from -800 to 800
- conv_weight: bfloat16 [3, 3, 640, 640], replicated, may hold values from -0.078125 to 0.078125
- conv_bias: float32 [640], replicated, may hold values from -4 to 4
- conv_gain: float32 [640], replicated, may hold values from 0.25 to 1.75
- temporal_gain: float32 [640], replicated, may hold values from 0.25 to 1.75
- temporal_query: bfloat16 [640, 640], replicated, may hold values from -18 to 18
- temporal_key: bfloat16 [640, 640], replicated, may hold values from -0.25 to 0.25
- temporal_value: bfloat16 [640, 640], replicated, may hold values from -0.25 to 0.25
- temporal_out: bfloat16 [640, 640], replicated, may hold values from -0.25 to 0.25
- cross_gain: float32 [640], replicated, may hold values from 0.25 to 1.75
- cross_query: bfloat16 [640, 640], replicated, may hold values from -0.25 to 0.25
- cross_out: bfloat16 [640, 640], replicated, may hold values from -0.25 to 0.25
Outputs:
- guided: bfloat16 [16, 16, 2, 14, 640], P('req', 'strip')
The draws below stay inside these ranges and needn't reach their ends.
Inputs may be any that keep to these rules, and one draw needn't show every extreme that they name: Requests 2 * i to 2 * i + 1 lie on req device i. Devices i and i + 4 form a pair, and of the 4 requests of a pair exactly 2 have gate 1. `context_slot`: A permutation of the 16 pages; page p lies on req device p // 2, and the page of a request lies on the request's own device or on the other device of its pair.
All inputs are finite; a program needn't handle non-finite values.
Results may differ from the reference program's by a relative error of at most 0.012.
Values may be sent and summed in bfloat16 or wider, within the bound.
No kernel may reach another device: no remote copies, remote signals or barrier semaphores. Data moves between devices by JAX's collectives and lax.ppermute only.
A program may use at most 64 MiB of HBM per device.

```python
import math
import jax
import jax.numpy as jnp
from jax import lax

C = 640
HEAD_DIM = 64
FRAMES = 14
REQ_DEV = 2
COLS = 2
CTX = 77
REQUESTS = 16
ROWS = 16


def pair_orders(key):
    pairs = REQUESTS // (2 * REQ_DEV)
    return jax.vmap(lambda one_key: jax.random.permutation(one_key, 2 * REQ_DEV))(jax.random.split(key, pairs))


def draw_gate(key, part):
    key = jax.random.fold_in(key, 11)
    orders = pair_orders(key)
    live = (orders < REQ_DEV).astype(jnp.int32)
    return jnp.stack([live[:, :REQ_DEV], live[:, REQ_DEV:]]).reshape(REQUESTS)


def draw_context_slot(key, part):
    key = jax.random.fold_in(key, 12)
    orders = pair_orders(key)
    pairs = REQUESTS // (2 * REQ_DEV)
    pair_ids = jnp.arange(pairs, dtype=jnp.int32)[:, None]
    lower = pair_ids * REQ_DEV + orders
    upper = (pair_ids + pairs) * REQ_DEV + orders - REQ_DEV
    slots = jnp.where(orders < REQ_DEV, lower, upper).astype(jnp.int32)
    return jnp.stack([slots[:, :REQ_DEV], slots[:, REQ_DEV:]]).reshape(REQUESTS)


def draw_hidden_states(key, part):
    key = jax.random.fold_in(key, 13)
    first_key = jax.random.fold_in(key, 0)
    shape = (2, REQUESTS, ROWS, COLS, FRAMES, C)
    values = jnp.clip(jax.random.normal(first_key, shape, jnp.float32), -6.0, 6.0)
    return values.astype(jnp.bfloat16)


def draw_context_pages(key, part):
    key = jax.random.fold_in(key, 14)
    first_key = jax.random.fold_in(key, 0)
    shape = (2, REQUESTS, CTX, C)
    values = jnp.clip(jax.random.normal(first_key, shape, jnp.float32), -4.0, 4.0)
    return values.astype(jnp.bfloat16)


def draw_temporal_query(key, part):
    key = jax.random.fold_in(key, 15)
    first_key = jax.random.fold_in(key, 0)
    values = jnp.clip(jax.random.normal(first_key, (C, C), jnp.float32), -4.0, 4.0) / math.sqrt(C)
    return values.astype(jnp.bfloat16)


def centred(rng, shape, spread, bound, kind=jnp.bfloat16):
    result = spread * jax.random.normal(rng, shape, jnp.float32)
    return jnp.clip(result, min=-bound, max=bound).astype(kind)


def setup_inputs(seed: int = 0) -> dict:
    splits = jax.random.split(jax.random.key(seed), 16)
    hidden_states = draw_hidden_states(jax.random.fold_in(splits[15], 71), 0)
    gate = draw_gate(jax.random.fold_in(splits[15], 71), 0)
    context_slot = draw_context_slot(jax.random.fold_in(splits[15], 71), 0)
    context_pages = draw_context_pages(jax.random.fold_in(splits[15], 71), 0)
    conv_weight = centred(splits[4], (3, 3, C, C), (9 * C) ** -0.5, 0.078125)
    conv_bias = centred(splits[5], (C,), 0.3, 4.0, jnp.float32)
    conv_gain = jnp.clip(1.0 + 0.15 * jax.random.normal(splits[6], (C,), jnp.float32), 0.25, 1.75)
    temporal_gain = jnp.clip(1.0 + 0.15 * jax.random.normal(splits[7], (C,), jnp.float32), 0.25, 1.75)
    temporal_query = draw_temporal_query(jax.random.fold_in(splits[15], 71), 0)
    temporal_key = centred(splits[9], (C, C), C ** -0.5, 0.25)
    temporal_value = centred(splits[10], (C, C), C ** -0.5, 0.25)
    temporal_out = centred(splits[11], (C, C), C ** -0.5, 0.25)
    cross_gain = jnp.clip(1.0 + 0.15 * jax.random.normal(splits[12], (C,), jnp.float32), 0.25, 1.75)
    cross_query = centred(splits[13], (C, C), C ** -0.5, 0.25)
    cross_out = centred(splits[14], (C, C), C ** -0.5, 0.25)
    return dict(hidden_states=hidden_states, gate=gate, context_slot=context_slot, context_pages=context_pages, conv_weight=conv_weight, conv_bias=conv_bias, conv_gain=conv_gain, temporal_gain=temporal_gain, temporal_query=temporal_query, temporal_key=temporal_key, temporal_value=temporal_value, temporal_out=temporal_out, cross_gain=cross_gain, cross_query=cross_query, cross_out=cross_out)


EPSILON = 1e-06

def rms_norm(field, scale_gain):
    field = field.astype(jnp.float32)
    return field * lax.rsqrt(lax.optimization_barrier(jnp.mean(field * field, axis=-1, keepdims=True)) + EPSILON) * scale_gain

def project(field, weight):
    return jnp.dot(field, weight, preferred_element_type=jnp.float32)

def branch_block(states, key_page, value_page, weights, with_cross):
    conv_weight, conv_bias, conv_gain, temporal_gain, temporal_query, temporal_key, temporal_value, temporal_out, cross_gain, cross_query, cross_out = weights
    rows, cols, frames, width = states.shape
    heads = width // HEAD_DIM
    activated = jax.nn.silu(rms_norm(states, conv_gain)).astype(jnp.bfloat16)
    padded = jnp.pad(activated, ((1, 1), (1, 1), (0, 0), (0, 0)))
    conv_sum = jnp.zeros(states.shape, jnp.float32) + conv_bias
    for row_step in range(3):
        for col_step in range(3):
            window = padded[row_step:row_step + rows, col_step:col_step + cols]
            conv_sum = conv_sum + project(window, conv_weight[row_step, col_step])
    after_conv = states.astype(jnp.float32) + conv_sum
    normed = rms_norm(after_conv, temporal_gain).astype(jnp.bfloat16)
    head_shape = (rows, cols, frames, heads, HEAD_DIM)
    time_query = project(normed, temporal_query).astype(jnp.bfloat16).reshape(head_shape)
    time_key = project(normed, temporal_key).astype(jnp.bfloat16).reshape(head_shape)
    time_value = project(normed, temporal_value).astype(jnp.bfloat16).reshape(head_shape)
    scores = jnp.einsum('rwfhd,rwghd->rwhfg', time_query.astype(jnp.float32), time_key.astype(jnp.float32)) * 0.125
    time_weights = jax.nn.softmax(scores, axis=-1).astype(jnp.bfloat16)
    time_mixed = jnp.einsum('rwhfg,rwghd->rwfhd', time_weights.astype(jnp.float32), time_value.astype(jnp.float32))
    time_mixed = time_mixed.astype(jnp.bfloat16).reshape(states.shape)
    after_time = after_conv + project(time_mixed, temporal_out)
    if with_cross:
        normed_cross = rms_norm(after_time, cross_gain).astype(jnp.bfloat16)
        queries = project(normed_cross, cross_query).astype(jnp.bfloat16).reshape(rows * cols * frames, heads, HEAD_DIM)
        key_heads = key_page.reshape(key_page.shape[0], heads, HEAD_DIM)
        value_heads = value_page.reshape(value_page.shape[0], heads, HEAD_DIM)
        cross_scores = jnp.einsum('phd,chd->hpc', queries.astype(jnp.float32), key_heads.astype(jnp.float32)) * 0.125
        cross_weights = jax.nn.softmax(cross_scores, axis=-1).astype(jnp.bfloat16)
        cross_mixed = jnp.einsum('hpc,chd->phd', cross_weights.astype(jnp.float32), value_heads.astype(jnp.float32))
        cross_mixed = cross_mixed.astype(jnp.bfloat16).reshape(states.shape)
        after_time = after_time + project(cross_mixed, cross_out)
    return after_time.astype(jnp.bfloat16)

def reference(hidden_states, gate, context_slot, context_pages, conv_weight, conv_bias, conv_gain, temporal_gain, temporal_query, temporal_key, temporal_value, temporal_out, cross_gain, cross_query, cross_out):
    weights = (conv_weight, conv_bias, conv_gain, temporal_gain, temporal_query, temporal_key, temporal_value, temporal_out, cross_gain, cross_query, cross_out)
    frame_scale = (1.0 + 2.0 * jnp.arange(FRAMES, dtype=jnp.float32) / (FRAMES - 1)).reshape(1, 1, FRAMES, 1)

    def one_request(request):
        page = context_slot[request]
        key_page = context_pages[0, page]
        value_page = context_pages[1, page]
        conditioned = branch_block(hidden_states[0, request], key_page, value_page, weights, True).astype(jnp.float32)
        unconditioned = branch_block(hidden_states[1, request], key_page, value_page, weights, False).astype(jnp.float32)
        mixed_out = unconditioned + frame_scale * (conditioned - unconditioned)
        return jnp.where(gate[request] == 1, mixed_out, conditioned).astype(jnp.bfloat16)
    return lax.map(one_request, jnp.arange(REQUESTS, dtype=jnp.int32))
```

```python
import functools
import jax
import jax.numpy as jnp
from jax import lax
from jax.experimental import pallas as pl
from jax.experimental.pallas import tpu as pltpu
from jax.sharding import PartitionSpec as P

HEAD_DIM = 64
REQ_DEV = 2
PAD = 16
EPSILON = 1e-06
LOG2E = 1.4426950408889634
F32 = jnp.float32
BF16 = jnp.bfloat16
NEG = -1e30


def rms(x, gain):
    return x * lax.rsqrt(jnp.mean(x * x, axis=-1, keepdims=True) + EPSILON) * gain


def silu(y):
    return y * (0.5 * jnp.tanh(0.5 * y) + 0.5)


def dot(a, b):
    return jnp.dot(a, b, preferred_element_type=F32)


def dot_t(a, b):
    return lax.dot_general(a, b, (((1,), (1,)), ((), ())), preferred_element_type=F32)


def conv_kernel(x_ref, w_ref, bias_ref, gain_ref, out_ref, act):
    slots, rows, _, wide = x_ref.shape
    width = wide // 2
    for c in range(2):
        x = x_ref[:, :, :, c * width : (c + 1) * width].astype(F32)
        act[:, :, :, c * width : (c + 1) * width] = silu(rms(x, gain_ref[...])).astype(BF16)
    for c in range(2):
        lo, hi = 1 - c, 3 - c

        def taps(dr):
            return w_ref[dr, lo:hi].reshape(wide, width)

        mid = dot(act[...].reshape(-1, wide), taps(1)).reshape(slots, rows, PAD, width)
        out_ref[c] = x_ref[:, :, :, c * width : (c + 1) * width].astype(F32) + bias_ref[...] + mid
        up = dot(act[:, : rows - 1].reshape(-1, wide), taps(0))
        out_ref[c, :, 1:] += up.reshape(slots, rows - 1, PAD, width)
        down = dot(act[:, 1:].reshape(-1, wide), taps(2))
        out_ref[c, :, : rows - 1] += down.reshape(slots, rows - 1, PAD, width)


def two_heads(q, k, v, mask, frames_scale):
    m = q.shape[0]
    n = k.shape[0]
    lane = lax.broadcasted_iota(jnp.int32, (m, 2 * HEAD_DIM), 1)
    first = lane < HEAD_DIM
    zero = jnp.zeros_like(q)
    stacked = jnp.concatenate([jnp.where(first, q, zero), jnp.where(first, zero, q)], axis=0)
    s = dot_t(stacked, k)
    if mask is not None:
        s = s + mask
    top = jnp.max(s, axis=-1, keepdims=True)
    p = jnp.exp2((s - top) * frames_scale).astype(BF16)
    both = dot(p, jnp.concatenate([v, jnp.ones((n, 2 * HEAD_DIM), BF16)], axis=1))
    d = 2 * HEAD_DIM
    num = jnp.where(first, both[:m, :d], both[m:, :d])
    den = jnp.where(first, both[:m, d:], both[m:, d:])
    return (num / den).astype(BF16)


def time_kernel(
    frames, part_ref, low_ref, high_ref, w_ref, cgain_ref, tgain_ref, wq_ref, wk_ref, wv_ref, wo_ref,
    xgain_ref, xq_ref, after_ref, query_ref, normed, tq, tk, tv, mixed, mask
):
    cols, slots, rows, _, width = part_ref.shape
    wide = 2 * width
    half = slots // 2
    total = cols * slots * rows * PAD
    block = half * rows * PAD
    low = jnp.concatenate(
        [silu(rms(low_ref[:, :, c * width : (c + 1) * width].astype(F32), cgain_ref[...])).astype(BF16) for c in range(2)],
        axis=-1,
    ).reshape(-1, wide)
    high = jnp.concatenate(
        [silu(rms(high_ref[:, :, c * width : (c + 1) * width].astype(F32), cgain_ref[...])).astype(BF16) for c in range(2)],
        axis=-1,
    ).reshape(-1, wide)
    for c in range(2):
        lo, hi = 1 - c, 3 - c
        after_ref[c] = part_ref[c]
        after_ref[c, :, 0] += dot(low, w_ref[0, lo:hi].reshape(wide, width)).reshape(slots, PAD, width)
        after_ref[c, :, rows - 1] += dot(high, w_ref[2, lo:hi].reshape(wide, width)).reshape(slots, PAD, width)
    normed[...] = rms(after_ref[...].reshape(total, width), tgain_ref[...]).astype(BF16)
    tq[...] = dot(normed[...], wq_ref[...]).astype(BF16)
    tk[...] = dot(normed[...], wk_ref[...]).astype(BF16)
    tv[...] = dot(normed[...], wv_ref[...]).astype(BF16)
    row = lax.broadcasted_iota(jnp.int32, (2 * block, block), 0) % block
    col = lax.broadcasted_iota(jnp.int32, (2 * block, block), 1)
    mask[...] = jnp.where((row // PAD == col // PAD) & (col % PAD < frames), 0.0, NEG).astype(F32)
    for b in range(total // block):
        rs = slice(b * block, (b + 1) * block)
        for j in range(width // 128):
            ls = slice(j * 128, (j + 1) * 128)
            mixed[rs, ls] = two_heads(tq[rs, ls], tk[rs, ls], tv[rs, ls], mask[...], 0.125 * LOG2E)
    after_ref[...] += dot(mixed[...], wo_ref[...]).reshape(after_ref.shape)
    for c in range(2):
        nc = rms(after_ref[c, :half].reshape(block, width), xgain_ref[...]).astype(BF16)
        query_ref[c] = dot(nc, xq_ref[...]).astype(BF16).reshape(half, rows, PAD, width)


def cross_kernel(
    frames, slot_ref, gate_ref, after_ref, query_ref, own_ref, far_ref, xo_ref, out_ref, mixed
):
    cols, slots, rows, _, width = after_ref.shape
    half = slots // 2
    for r in range(half):
        index = slot_ref[r]
        mine = index < REQ_DEV
        i = lax.rem(index, REQ_DEV)
        k = jnp.where(mine, own_ref[0, i], far_ref[0, i])
        v = jnp.where(mine, own_ref[1, i], far_ref[1, i])
        q = query_ref[:, r].reshape(cols * rows * PAD, width)
        for j in range(width // 128):
            ls = slice(j * 128, (j + 1) * 128)
            out = two_heads(q[:, ls], k[:, ls], v[:, ls], None, 0.125 * LOG2E)
            mixed[:, r, :, :, ls] = out.reshape(cols, rows, PAD, 128)
    frame = lax.broadcasted_iota(jnp.int32, (rows, PAD, width), 1).astype(F32)
    scale = 1.0 + 2.0 * frame / (frames - 1)
    for c in range(cols):
        add = dot(mixed[c].reshape(-1, width), xo_ref[...]).reshape(half, rows, PAD, width)
        for r in range(half):
            cond = (after_ref[c, r] + add[r]).astype(BF16).astype(F32)
            uncond = after_ref[c, half + r].astype(BF16).astype(F32)
            guided = jnp.where(gate_ref[r] == 1, uncond + scale * (cond - uncond), cond)
            out_ref[r, :, :, c * width : (c + 1) * width] = guided.astype(BF16)


def on_device(
    hidden_states, gate, context_slot, context_pages, conv_weight, conv_bias, conv_gain, temporal_gain,
    temporal_query, temporal_key, temporal_value, temporal_out, cross_gain, cross_query, cross_out,
):
    _, _, rows, cols, frames, width = hidden_states.shape
    slots = 2 * REQ_DEV
    count = lax.axis_size("req")
    device_index = lax.axis_index("req")
    partner_pairs = [(i, i ^ (count // 2)) for i in range(count)]
    strips = lax.axis_size("strip")
    forward = [(i, i + 1) for i in range(strips - 1)]
    backward = [(i + 1, i) for i in range(strips - 1)]
    wanted = lax.dynamic_slice_in_dim(context_slot, device_index * REQ_DEV, REQ_DEV)
    local = wanted - device_index * REQ_DEV
    index = jnp.where((local >= 0) & (local < REQ_DEV), local, REQ_DEV + lax.rem(wanted, REQ_DEV))

    far_pages = lax.ppermute(context_pages, "req", partner_pairs)
    x = hidden_states.reshape((slots, rows, cols, frames, width)).transpose(0, 1, 3, 2, 4)
    x = x.reshape(slots, rows, frames, cols * width)
    x = jnp.pad(x, ((0, 0), (0, 0), (0, PAD - frames), (0, 0)))
    low = lax.ppermute(x[:, rows - 1], "strip", forward)
    high = lax.ppermute(x[:, 0], "strip", backward)

    vec = lambda g: g.reshape(1, width)
    vm = pl.BlockSpec(memory_space=pltpu.VMEM)
    sm = pl.BlockSpec(memory_space=pltpu.SMEM)
    any_ = pl.BlockSpec(memory_space=pl.ANY)
    total = cols * slots * rows * PAD
    part = pl.pallas_call(
        conv_kernel,
        out_shape=jax.ShapeDtypeStruct((cols, slots, rows, PAD, width), F32),
        in_specs=[vm] * 4,
        out_specs=vm,
        scratch_shapes=[pltpu.VMEM((slots, rows, PAD, cols * width), BF16)],
        compiler_params=pltpu.CompilerParams(vmem_limit_bytes=24 << 20),
        cost_estimate=pl.CostEstimate(flops=2 * 256 * 3840 * 640 * 2, bytes_accessed=9 << 20, transcendentals=0),
        name="conv_own",
    )(x, conv_weight, vec(conv_bias), vec(conv_gain))
    after, query = pl.pallas_call(
        functools.partial(time_kernel, frames),
        out_shape=(
            jax.ShapeDtypeStruct((cols, slots, rows, PAD, width), F32),
            jax.ShapeDtypeStruct((cols, REQ_DEV, rows, PAD, width), BF16),
        ),
        in_specs=[vm] * 12,
        out_specs=(vm, vm),
        scratch_shapes=[pltpu.VMEM((total, width), BF16)] * 5
        + [pltpu.VMEM((slots * rows * PAD, slots * rows * PAD // 2), F32)],
        compiler_params=pltpu.CompilerParams(vmem_limit_bytes=32 << 20),
        cost_estimate=pl.CostEstimate(flops=2 * 512 * 640 * 640 * 5, bytes_accessed=9 << 20, transcendentals=0),
        name="time_mix",
    )(
        part, low, high, conv_weight, vec(conv_gain), vec(temporal_gain), temporal_query, temporal_key,
        temporal_value, temporal_out, vec(cross_gain), cross_query,
    )
    out = pl.pallas_call(
        functools.partial(cross_kernel, frames),
        out_shape=jax.ShapeDtypeStruct((REQ_DEV, rows, PAD, cols * width), BF16),
        in_specs=[sm, sm] + [vm] * 5,
        out_specs=vm,
        scratch_shapes=[pltpu.VMEM((cols, REQ_DEV, rows, PAD, width), BF16)],
        compiler_params=pltpu.CompilerParams(vmem_limit_bytes=24 << 20),
        cost_estimate=pl.CostEstimate(flops=2 * 256 * 640 * 640, bytes_accessed=4 << 20, transcendentals=0),
        name="cross_mix",
    )(index, gate, after, query, context_pages, far_pages, cross_out)
    out = out[:, :, :frames].reshape(REQ_DEV, rows, frames, cols, width)
    return out.transpose(0, 1, 3, 2, 4)


def solution(mesh):
    return jax.shard_map(
        on_device,
        mesh=mesh,
        in_specs=(
            P(None, "req", "strip", None, None, None),
            P("req"),
            P(),
            P(None, "req", None, None),
        )
        + (P(),) * 11,
        out_specs=P("req", "strip", None, None, None),
        check_vma=False,
    )
```

```python
import functools
import jax
import jax.numpy as jnp
from jax import lax
from jax.experimental import pallas as pl
from jax.experimental.pallas import tpu as pltpu
from jax.sharding import PartitionSpec as P

HEAD_DIM = 64
REQ_DEV = 2
PAD = 16
EPSILON = 1e-06
LOG2E = 1.4426950408889634
F32 = jnp.float32
BF16 = jnp.bfloat16
NEG = -1e30
COST0, COST1, COST2, COST3 = 12 * 10**9, 10**9, 10**9, 10**9


def rms(x, gain):
    return x * lax.rsqrt(jnp.mean(x * x, axis=-1, keepdims=True) + EPSILON) * gain.reshape((1,) * (x.ndim - 1) + (-1,))


def silu(y):
    return y * (0.5 * jnp.tanh(0.5 * y) + 0.5)


def dot(a, b):
    return jnp.dot(a, b, preferred_element_type=F32)


def dot_t(a, b):
    return lax.dot_general(a, b, (((1,), (1,)), ((), ())), preferred_element_type=F32)


def act_kernel(raw_ref, gain_ref, x_ref, act_ref, first_ref, last_ref):
    slots, rows, frames, cols, width = raw_ref.shape
    for s in range(slots):
        for c in range(cols):
            ls = slice(c * width, (c + 1) * width)
            for r in range(rows):
                raw = raw_ref[s, r, :, c, :]
                raw = jnp.concatenate([raw, jnp.zeros((PAD - frames, width), BF16)], axis=0)
                x_ref[s, r, :, ls] = raw
                a = silu(rms(raw.astype(F32), gain_ref[...])).astype(BF16)
                act_ref[s, r, :, ls] = a
                if r == 0:
                    first_ref[s, :, ls] = a
                if r == rows - 1:
                    last_ref[s, :, ls] = a


def conv_kernel(x_ref, act, w_ref, bias_ref, out_ref):
    slots, rows, _, wide = x_ref.shape
    width = wide // 2
    for c in range(2):
        lo, hi = 1 - c, 3 - c

        def taps(dr):
            return w_ref[dr, lo:hi].reshape(wide, width)

        mid = dot(act[...].reshape(-1, wide), taps(1)).reshape(slots, rows, PAD, width)
        out_ref[c] = x_ref[:, :, :, c * width : (c + 1) * width].astype(F32) + bias_ref[...].reshape(1, 1, 1, width) + mid
        up = dot(act[:, : rows - 1].reshape(-1, wide), taps(0))
        out_ref[c, :, 1:] += up.reshape(slots, rows - 1, PAD, width)
        down = dot(act[:, 1:].reshape(-1, wide), taps(2))
        out_ref[c, :, : rows - 1] += down.reshape(slots, rows - 1, PAD, width)


def two_heads(q, k, v, mask, frames_scale):
    m = q.shape[0]
    n = k.shape[0]
    lane = lax.broadcasted_iota(jnp.int32, (m, 2 * HEAD_DIM), 1)
    first = lane < HEAD_DIM
    zero = jnp.zeros_like(q)
    stacked = jnp.concatenate([jnp.where(first, q, zero), jnp.where(first, zero, q)], axis=0)
    s = dot_t(stacked, k)
    if mask is not None:
        s = s + mask
    top = jnp.max(s, axis=-1, keepdims=True)
    p = jnp.exp2((s - top) * frames_scale).astype(BF16)
    both = dot(p, jnp.concatenate([v, jnp.ones((n, 2 * HEAD_DIM), BF16)], axis=1))
    d = 2 * HEAD_DIM
    num = jnp.where(first, both[:m, :d], both[m:, :d])
    den = jnp.where(first, both[:m, d:], both[m:, d:])
    return (num / den).astype(BF16)


def time_kernel(
    frames, part_ref, low_ref, high_ref, w_ref, tgain_ref, wq_ref, wk_ref, wv_ref, wo_ref,
    xgain_ref, xq_ref, after_ref, query_ref, normed, tq, tk, tv, mixed, mask
):
    cols, slots, rows, _, width = part_ref.shape
    wide = 2 * width
    half = slots // 2
    total = cols * slots * rows * PAD
    block = half * rows * PAD
    low = low_ref[...].reshape(-1, wide)
    high = high_ref[...].reshape(-1, wide)
    for c in range(2):
        lo, hi = 1 - c, 3 - c
        after_ref[c] = part_ref[c]
        after_ref[c, :, 0] += dot(low, w_ref[0, lo:hi].reshape(wide, width)).reshape(slots, PAD, width)
        after_ref[c, :, rows - 1] += dot(high, w_ref[2, lo:hi].reshape(wide, width)).reshape(slots, PAD, width)
    normed[...] = rms(after_ref[...].reshape(total, width), tgain_ref[...]).astype(BF16)
    tq[...] = dot(normed[...], wq_ref[...]).astype(BF16)
    tk[...] = dot(normed[...], wk_ref[...]).astype(BF16)
    tv[...] = dot(normed[...], wv_ref[...]).astype(BF16)
    row = lax.broadcasted_iota(jnp.int32, (2 * block, block), 0) % block
    col = lax.broadcasted_iota(jnp.int32, (2 * block, block), 1)
    mask[...] = jnp.where((row // PAD == col // PAD) & (col % PAD < frames), 0.0, NEG).astype(F32)
    for b in range(total // block):
        rs = slice(b * block, (b + 1) * block)
        for j in range(width // 128):
            ls = slice(j * 128, (j + 1) * 128)
            mixed[rs, ls] = two_heads(tq[rs, ls], tk[rs, ls], tv[rs, ls], mask[...], 0.125 * LOG2E)
    after_ref[...] += dot(mixed[...], wo_ref[...]).reshape(after_ref.shape)
    for c in range(2):
        nc = rms(after_ref[c, :half].reshape(block, width), xgain_ref[...]).astype(BF16)
        query_ref[c] = dot(nc, xq_ref[...]).astype(BF16).reshape(half, rows, PAD, width)


def cross_kernel(
    frames, slot_ref, gate_ref, after_ref, query_ref, own_ref, far_ref, xo_ref, out_ref, mixed
):
    cols, slots, rows, _, width = after_ref.shape
    half = slots // 2
    first_page = lax.axis_index("req") * REQ_DEV
    for r in range(half):
        page = slot_ref[first_page + r]
        i = lax.rem(page, REQ_DEV)
        mine = page - i == first_page
        k = jnp.where(mine, own_ref[0, i], far_ref[0, i])
        v = jnp.where(mine, own_ref[1, i], far_ref[1, i])
        q = query_ref[:, r].reshape(cols * rows * PAD, width)
        for j in range(width // 128):
            ls = slice(j * 128, (j + 1) * 128)
            out = two_heads(q[:, ls], k[:, ls], v[:, ls], None, 0.125 * LOG2E)
            mixed[:, r, :, :, ls] = out.reshape(cols, rows, PAD, 128)
    frame = lax.broadcasted_iota(jnp.int32, (rows, PAD, width), 1).astype(F32)
    scale = 1.0 + 2.0 * frame / (frames - 1)
    for c in range(cols):
        add = dot(mixed[c].reshape(-1, width), xo_ref[...]).reshape(half, rows, PAD, width)
        for r in range(half):
            cond = (after_ref[c, r] + add[r]).astype(BF16).astype(F32)
            uncond = after_ref[c, half + r].astype(BF16).astype(F32)
            guided = jnp.where(gate_ref[r] == 1, uncond + scale * (cond - uncond), cond)
            out_ref[r, :, :, c * width : (c + 1) * width] = guided.astype(BF16)


def on_device(
    hidden_states, gate, context_slot, context_pages, conv_weight, conv_bias, conv_gain, temporal_gain,
    temporal_query, temporal_key, temporal_value, temporal_out, cross_gain, cross_query, cross_out,
):
    _, _, rows, cols, frames, width = hidden_states.shape
    slots = 2 * REQ_DEV
    count = lax.axis_size("req")
    partner_pairs = [(i, i ^ (count // 2)) for i in range(count)]
    strips = lax.axis_size("strip")
    forward = [(i, i + 1) for i in range(strips - 1)]
    backward = [(i + 1, i) for i in range(strips - 1)]
    far_pages = lax.ppermute(context_pages, "req", partner_pairs)
    vm = pl.BlockSpec(memory_space=pltpu.VMEM)
    sm = pl.BlockSpec(memory_space=pltpu.SMEM)
    any_ = pl.BlockSpec(memory_space=pl.ANY)
    total = cols * slots * rows * PAD
    wide = cols * width
    raw = hidden_states.reshape((slots, rows, cols, frames, width)).transpose(0, 1, 3, 2, 4)
    x, act, first, last = pl.pallas_call(
        act_kernel,
        out_shape=(
            jax.ShapeDtypeStruct((slots, rows, PAD, wide), BF16),
            jax.ShapeDtypeStruct((slots, rows, PAD, wide), BF16),
            jax.ShapeDtypeStruct((slots, PAD, wide), BF16),
            jax.ShapeDtypeStruct((slots, PAD, wide), BF16),
        ),
        in_specs=[vm] * 2,
        out_specs=(vm,) * 4,
        compiler_params=pltpu.CompilerParams(vmem_limit_bytes=8 << 20),
        cost_estimate=pl.CostEstimate(flops=COST0, bytes_accessed=0, transcendentals=0),
        name="activate",
    )(raw, conv_gain)
    low = lax.ppermute(last, "strip", forward)
    high = lax.ppermute(first, "strip", backward)
    part = pl.pallas_call(
        conv_kernel,
        out_shape=jax.ShapeDtypeStruct((cols, slots, rows, PAD, width), F32),
        in_specs=[vm] * 4,
        out_specs=vm,
        compiler_params=pltpu.CompilerParams(vmem_limit_bytes=16 << 20),
        cost_estimate=pl.CostEstimate(flops=COST1, bytes_accessed=0, transcendentals=0),
        name="conv_own",
    )(x, act, conv_weight, conv_bias)
    after, query = pl.pallas_call(
        functools.partial(time_kernel, frames),
        out_shape=(
            jax.ShapeDtypeStruct((cols, slots, rows, PAD, width), F32),
            jax.ShapeDtypeStruct((cols, REQ_DEV, rows, PAD, width), BF16),
        ),
        in_specs=[vm] * 11,
        out_specs=(vm, vm),
        scratch_shapes=[pltpu.VMEM((total, width), BF16)] * 5
        + [
            pltpu.VMEM((slots * rows * PAD, slots * rows * PAD // 2), F32),
        ],
        compiler_params=pltpu.CompilerParams(vmem_limit_bytes=16 << 20),
        cost_estimate=pl.CostEstimate(flops=COST2, bytes_accessed=0, transcendentals=0),
        name="time_mix",
    )(
        part, low, high, conv_weight, temporal_gain, temporal_query, temporal_key,
        temporal_value, temporal_out, cross_gain, cross_query,
    )
    out = pl.pallas_call(
        functools.partial(cross_kernel, frames),
        out_shape=jax.ShapeDtypeStruct((REQ_DEV, rows, PAD, cols * width), BF16),
        in_specs=[sm, sm] + [vm] * 5,
        out_specs=vm,
        scratch_shapes=[pltpu.VMEM((cols, REQ_DEV, rows, PAD, width), BF16)],
        compiler_params=pltpu.CompilerParams(vmem_limit_bytes=8 << 20),
        cost_estimate=pl.CostEstimate(flops=COST3, bytes_accessed=0, transcendentals=0),
        name="cross_mix",
    )(context_slot, gate, after, query, context_pages, far_pages, cross_out)
    out = out[:, :, :frames].reshape(REQ_DEV, rows, frames, cols, width)
    return out.transpose(0, 1, 3, 2, 4)


def solution(mesh):
    return jax.shard_map(
        on_device,
        mesh=mesh,
        in_specs=(
            P(None, "req", "strip", None, None, None),
            P("req"),
            P(),
            P(None, "req", None, None),
        )
        + (P(),) * 11,
        out_specs=P("req", "strip", None, None, None),
        check_vma=False,
    )
```

```python
import functools
import jax
import jax.numpy as jnp
from jax import lax
from jax.experimental import pallas as pl
from jax.experimental.pallas import tpu as pltpu
from jax.sharding import PartitionSpec as P

HEAD_DIM = 64
REQ_DEV = 2
PAD = 16
EPSILON = 1e-06
LOG2E = 1.4426950408889634
F32 = jnp.float32
BF16 = jnp.bfloat16
NEG = -1e30
COSTP, COST0, COST1, COST2, COST3 = 3 * 10**9, 16 * 10**9, 10**9, 10**9, 10**9


def cost(flops):
    return pl.CostEstimate(flops=flops, bytes_accessed=0, transcendentals=0)


def rms(x, gain):
    return x * lax.rsqrt(jnp.mean(x * x, axis=-1, keepdims=True) + EPSILON) * gain.reshape((1,) * (x.ndim - 1) + (-1,))


def silu(y):
    return y * (0.5 * jnp.tanh(0.5 * y) + 0.5)


def dot(a, b):
    return jnp.dot(a, b, preferred_element_type=F32)


def dot_t(a, b):
    return lax.dot_general(a, b, (((1,), (1,)), ((), ())), preferred_element_type=F32)


def pass_kernel(in_ref, out_ref):
    pass


def first_row():
    return 1 - lax.rem(lax.axis_index("strip"), 2)


def lay_out(raw_ref, gain_ref, s, r, c):
    frames, width = raw_ref.shape[2], raw_ref.shape[4]
    raw = raw_ref[s, r, :, c, :]
    raw = jnp.concatenate([raw, jnp.zeros((PAD - frames, width), BF16)], axis=0)
    return raw, silu(rms(raw.astype(F32), gain_ref[...])).astype(BF16)


def edge_kernel(raw_ref, gain_ref, x_ref, act_ref):
    slots, rows, _, cols, width = raw_ref.shape
    r = first_row() * (rows - 1)
    for s in range(slots):
        for c in range(cols):
            ls = slice(c * width, (c + 1) * width)
            x_ref[s, :, ls], act_ref[s, :, ls] = lay_out(raw_ref, gain_ref, s, r, c)


def act_kernel(raw_ref, gain_ref, edge_x_ref, edge_act_ref, x_ref, act_ref, edge_ref):
    slots, rows, _, cols, width = raw_ref.shape
    done = first_row() * (rows - 1)
    other = rows - 1 - done
    x_ref[:, done] = edge_x_ref[...]
    act_ref[:, done] = edge_act_ref[...]
    for s in range(slots):
        for c in range(cols):
            ls = slice(c * width, (c + 1) * width)
            for r in (other, *range(1, rows - 1)):
                x_ref[s, r, :, ls], a = lay_out(raw_ref, gain_ref, s, r, c)
                act_ref[s, r, :, ls] = a
                if r is other:
                    edge_ref[s, :, ls] = a


def conv_kernel(x_ref, act_ref, near_ref, w_ref, bias_ref, out_ref, ext):
    slots, rows, _, wide = x_ref.shape
    width = wide // 2
    side = 2 * first_row()
    ext[:, 1 : rows + 1] = act_ref[...]
    ext[:, side // 2 * (rows + 1)] = near_ref[...]
    both = jnp.concatenate(
        [ext[:, 1 : rows + 1].reshape(-1, wide), ext[:, pl.ds(side, rows)].reshape(-1, wide)], axis=-1
    )
    inner = ext[:, pl.ds(2 - side // 2, rows - 1)].reshape(-1, wide)
    inner_rows = pl.ds(side // 2, rows - 1)
    for c in range(2):
        taps = pl.ds(1 - c, 2)
        weights = jnp.concatenate(
            [w_ref[1, taps].reshape(wide, width), w_ref[side, taps].reshape(wide, width)], axis=0
        )
        mid = dot(both, weights).reshape(slots, rows, PAD, width)
        out_ref[c] = x_ref[:, :, :, c * width : (c + 1) * width].astype(F32) + bias_ref[...].reshape(1, 1, 1, width) + mid
        rest = dot(inner, w_ref[2 - side, taps].reshape(wide, width))
        out_ref[c, :, inner_rows] += rest.reshape(slots, rows - 1, PAD, width)


def two_heads(q, k, v, mask, frames_scale):
    m = q.shape[0]
    n = k.shape[0]
    lane = lax.broadcasted_iota(jnp.int32, (m, 2 * HEAD_DIM), 1)
    first = lane < HEAD_DIM
    zero = jnp.zeros_like(q)
    stacked = jnp.concatenate([jnp.where(first, q, zero), jnp.where(first, zero, q)], axis=0)
    s = dot_t(stacked, k)
    if mask is not None:
        s = s + mask
    top = jnp.max(s, axis=-1, keepdims=True)
    p = jnp.exp2((s - top) * frames_scale).astype(BF16)
    both = dot(p, jnp.concatenate([v, jnp.ones((n, 2 * HEAD_DIM), BF16)], axis=1))
    d = 2 * HEAD_DIM
    num = jnp.where(first, both[:m, :d], both[m:, :d])
    den = jnp.where(first, both[:m, d:], both[m:, d:])
    return (num / den).astype(BF16)


def time_kernel(
    frames, part_ref, next_ref, w_ref, tgain_ref, wq_ref, wk_ref, wv_ref, wo_ref,
    xgain_ref, xq_ref, after_ref, query_ref, normed, tq, tk, tv, mixed, mask
):
    cols, slots, rows, _, width = part_ref.shape
    wide = 2 * width
    half = slots // 2
    total = cols * slots * rows * PAD
    block = half * rows * PAD
    side = 1 - first_row()
    other = next_ref[...].reshape(-1, wide)
    for c in range(2):
        after_ref[c] = part_ref[c]
        add = dot(other, w_ref[2 * side, pl.ds(1 - c, 2)].reshape(wide, width))
        after_ref[c, :, side * (rows - 1)] += add.reshape(slots, PAD, width)
    normed[...] = rms(after_ref[...].reshape(total, width), tgain_ref[...]).astype(BF16)
    tq[...] = dot(normed[...], wq_ref[...]).astype(BF16)
    tk[...] = dot(normed[...], wk_ref[...]).astype(BF16)
    tv[...] = dot(normed[...], wv_ref[...]).astype(BF16)
    row = lax.broadcasted_iota(jnp.int32, (2 * block, block), 0) % block
    col = lax.broadcasted_iota(jnp.int32, (2 * block, block), 1)
    mask[...] = jnp.where((row // PAD == col // PAD) & (col % PAD < frames), 0.0, NEG).astype(F32)
    for b in range(total // block):
        rs = slice(b * block, (b + 1) * block)
        for j in range(width // 128):
            ls = slice(j * 128, (j + 1) * 128)
            mixed[rs, ls] = two_heads(tq[rs, ls], tk[rs, ls], tv[rs, ls], mask[...], 0.125 * LOG2E)
    after_ref[...] += dot(mixed[...], wo_ref[...]).reshape(after_ref.shape)
    for c in range(2):
        nc = rms(after_ref[c, :half].reshape(block, width), xgain_ref[...]).astype(BF16)
        query_ref[c] = dot(nc, xq_ref[...]).astype(BF16).reshape(half, rows, PAD, width)


def cross_kernel(
    frames, slot_ref, gate_ref, after_ref, query_ref, own_ref, far_ref, xo_ref, out_ref, mixed
):
    cols, slots, rows, _, width = after_ref.shape
    half = slots // 2
    first_page = lax.axis_index("req") * REQ_DEV
    for r in range(half):
        page = slot_ref[first_page + r]
        i = lax.rem(page, REQ_DEV)
        mine = page - i == first_page
        k = jnp.where(mine, own_ref[0, i], far_ref[0, i])
        v = jnp.where(mine, own_ref[1, i], far_ref[1, i])
        q = query_ref[:, r].reshape(cols * rows * PAD, width)
        for j in range(width // 128):
            ls = slice(j * 128, (j + 1) * 128)
            out = two_heads(q[:, ls], k[:, ls], v[:, ls], None, 0.125 * LOG2E)
            mixed[:, r, :, :, ls] = out.reshape(cols, rows, PAD, 128)
    frame = lax.broadcasted_iota(jnp.int32, (rows, PAD, width), 1).astype(F32)
    scale = 1.0 + 2.0 * frame / (frames - 1)
    for c in range(cols):
        add = dot(mixed[c].reshape(-1, width), xo_ref[...]).reshape(half, rows, PAD, width)
        for r in range(half):
            cond = (after_ref[c, r] + add[r]).astype(BF16).astype(F32)
            uncond = after_ref[c, half + r].astype(BF16).astype(F32)
            guided = jnp.where(gate_ref[r] == 1, uncond + scale * (cond - uncond), cond)
            out_ref[r, :, :, c * width : (c + 1) * width] = guided.astype(BF16)


def on_device(
    hidden_states, gate, context_slot, context_pages, conv_weight, conv_bias, conv_gain, temporal_gain,
    temporal_query, temporal_key, temporal_value, temporal_out, cross_gain, cross_query, cross_out,
):
    _, _, rows, cols, frames, width = hidden_states.shape
    slots = 2 * REQ_DEV
    count = lax.axis_size("req")
    partner_pairs = [(i, i ^ (count // 2)) for i in range(count)]
    strips = lax.axis_size("strip")
    near_pairs, next_pairs = (
        [p for i in range(start, strips - 1, 2) for p in ((i, i + 1), (i + 1, i))] for start in (0, 1)
    )

    vm = pl.BlockSpec(memory_space=pltpu.VMEM)
    sm = pl.BlockSpec(memory_space=pltpu.SMEM)
    any_ = pl.BlockSpec(memory_space=pl.ANY)
    total = cols * slots * rows * PAD
    wide = cols * width
    raw = hidden_states.reshape((slots, rows, cols, frames, width)).transpose(0, 1, 3, 2, 4)
    context_pages = pl.pallas_call(
        pass_kernel,
        out_shape=jax.ShapeDtypeStruct(context_pages.shape, BF16),
        in_specs=[any_],
        out_specs=any_,
        input_output_aliases={0: 0},
        cost_estimate=cost(COSTP),
        name="pages",
    )(context_pages)
    far_pages = lax.ppermute(context_pages, "req", partner_pairs)
    row = jax.ShapeDtypeStruct((slots, PAD, wide), BF16)
    whole = jax.ShapeDtypeStruct((slots, rows, PAD, wide), BF16)
    edge_x, edge_act = pl.pallas_call(
        edge_kernel,
        out_shape=(row, row),
        in_specs=[vm] * 2,
        out_specs=(vm, vm),
        compiler_params=pltpu.CompilerParams(vmem_limit_bytes=8 << 20),
        cost_estimate=cost(COST0),
        name="edge",
    )(raw, conv_gain)
    near = lax.ppermute(edge_act, "strip", near_pairs)
    x, act, edge = pl.pallas_call(
        act_kernel,
        out_shape=(whole, whole, row),
        in_specs=[vm] * 4,
        out_specs=(vm,) * 3,
        compiler_params=pltpu.CompilerParams(vmem_limit_bytes=8 << 20),
        cost_estimate=cost(COST1),
        name="activate",
    )(raw, conv_gain, edge_x, edge_act)
    other = lax.ppermute(edge, "strip", next_pairs)
    part = pl.pallas_call(
        conv_kernel,
        out_shape=jax.ShapeDtypeStruct((cols, slots, rows, PAD, width), F32),
        in_specs=[vm] * 5,
        out_specs=vm,
        scratch_shapes=[pltpu.VMEM((slots, rows + 2, PAD, wide), BF16)],
        compiler_params=pltpu.CompilerParams(vmem_limit_bytes=16 << 20),
        cost_estimate=cost(COST1),
        name="conv_own",
    )(x, act, near, conv_weight, conv_bias)
    after, query = pl.pallas_call(
        functools.partial(time_kernel, frames),
        out_shape=(
            jax.ShapeDtypeStruct((cols, slots, rows, PAD, width), F32),
            jax.ShapeDtypeStruct((cols, REQ_DEV, rows, PAD, width), BF16),
        ),
        in_specs=[vm] * 10,
        out_specs=(vm, vm),
        scratch_shapes=[pltpu.VMEM((total, width), BF16)] * 5
        + [
            pltpu.VMEM((slots * rows * PAD, slots * rows * PAD // 2), F32),
        ],
        compiler_params=pltpu.CompilerParams(vmem_limit_bytes=16 << 20),
        cost_estimate=cost(COST2),
        name="time_mix",
    )(
        part, other, conv_weight, temporal_gain, temporal_query, temporal_key,
        temporal_value, temporal_out, cross_gain, cross_query,
    )
    out = pl.pallas_call(
        functools.partial(cross_kernel, frames),
        out_shape=jax.ShapeDtypeStruct((REQ_DEV, rows, PAD, cols * width), BF16),
        in_specs=[sm, sm] + [vm] * 5,
        out_specs=vm,
        scratch_shapes=[pltpu.VMEM((cols, REQ_DEV, rows, PAD, width), BF16)],
        compiler_params=pltpu.CompilerParams(vmem_limit_bytes=8 << 20),
        cost_estimate=cost(COST3),
        name="cross_mix",
    )(context_slot, gate, after, query, context_pages, far_pages, cross_out)
    out = out[:, :, :frames].reshape(REQ_DEV, rows, frames, cols, width)
    return out.transpose(0, 1, 3, 2, 4)


def solution(mesh):
    return jax.shard_map(
        on_device,
        mesh=mesh,
        in_specs=(
            P(None, "req", "strip", None, None, None),
            P("req"),
            P(),
            P(None, "req", None, None),
        )
        + (P(),) * 11,
        out_specs=P("req", "strip", None, None, None),
        check_vma=False,
    )
```

```python
import functools
import jax
import jax.numpy as jnp
from jax import lax
from jax.experimental import pallas as pl
from jax.experimental.pallas import tpu as pltpu
from jax.sharding import PartitionSpec as P

HEAD_DIM = 64
REQ_DEV = 2
PAD = 16
EPSILON = 1e-06
LOG2E = 1.4426950408889634
F32 = jnp.float32
BF16 = jnp.bfloat16
NEG = -1e30
COSTP, COST0, COST1, COST2, COST3 = 3 * 10**9, 16 * 10**9, 3 * 10**8, 6 * 10**9, 10**9


def cost(flops):
    return pl.CostEstimate(flops=flops, bytes_accessed=0, transcendentals=0)


def rms(x, gain):
    return x * lax.rsqrt(jnp.mean(x * x, axis=-1, keepdims=True) + EPSILON) * gain.reshape((1,) * (x.ndim - 1) + (-1,))


def silu(y):
    return y * (0.5 * jnp.tanh(0.5 * y) + 0.5)


def dot(a, b):
    return jnp.dot(a, b, preferred_element_type=F32)


def dot_t(a, b):
    return lax.dot_general(a, b, (((1,), (1,)), ((), ())), preferred_element_type=F32)


def pages_kernel(pages_ref, half_ref, sem):
    copy = pltpu.make_async_copy(pages_ref.at[1 - first_row()], half_ref, sem)
    copy.start()
    copy.wait()


def first_row():
    return 1 - lax.rem(lax.axis_index("strip"), 2)


def lay_out(raw_ref, gain_ref, s, r, c):
    frames, width = raw_ref.shape[2], raw_ref.shape[4]
    raw = raw_ref[s, r, :, c, :]
    raw = jnp.concatenate([raw, jnp.zeros((PAD - frames, width), BF16)], axis=0)
    return raw, silu(rms(raw.astype(F32), gain_ref[...])).astype(BF16)


def edge_kernel(raw_ref, gain_ref, x_ref, act_ref):
    slots, rows, _, cols, width = raw_ref.shape
    r = first_row() * (rows - 1)
    for s in range(slots):
        for c in range(cols):
            ls = slice(c * width, (c + 1) * width)
            x_ref[s, :, ls], act_ref[s, :, ls] = lay_out(raw_ref, gain_ref, s, r, c)


def act_kernel(raw_ref, gain_ref, edge_x_ref, edge_act_ref, x_ref, act_ref, edge_ref):
    slots, rows, _, cols, width = raw_ref.shape
    done = first_row() * (rows - 1)
    other = rows - 1 - done
    x_ref[:, done] = edge_x_ref[...]
    act_ref[:, done] = edge_act_ref[...]
    for s in range(slots):
        for c in range(cols):
            ls = slice(c * width, (c + 1) * width)
            for r in (other, *range(1, rows - 1)):
                x_ref[s, r, :, ls], a = lay_out(raw_ref, gain_ref, s, r, c)
                act_ref[s, r, :, ls] = a
                if r is other:
                    edge_ref[s, :, ls] = a


def conv_kernel(x_ref, act_ref, near_ref, w_ref, bias_ref, out_ref, ext):
    slots, rows, _, wide = x_ref.shape
    width = wide // 2
    side = 2 * first_row()
    ext[:, 1 : rows + 1] = act_ref[...]
    ext[:, side // 2 * (rows + 1)] = near_ref[...]
    both = jnp.concatenate(
        [ext[:, 1 : rows + 1].reshape(-1, wide), ext[:, pl.ds(side, rows)].reshape(-1, wide)], axis=-1
    )
    inner = ext[:, pl.ds(2 - side // 2, rows - 1)].reshape(-1, wide)
    inner_rows = pl.ds(side // 2, rows - 1)
    for c in range(2):
        taps = pl.ds(1 - c, 2)
        weights = jnp.concatenate(
            [w_ref[1, taps].reshape(wide, width), w_ref[side, taps].reshape(wide, width)], axis=0
        )
        mid = dot(both, weights).reshape(slots, rows, PAD, width)
        out_ref[c] = x_ref[:, :, :, c * width : (c + 1) * width].astype(F32) + bias_ref[...].reshape(1, 1, 1, width) + mid
        rest = dot(inner, w_ref[2 - side, taps].reshape(wide, width))
        out_ref[c, :, inner_rows] += rest.reshape(slots, rows - 1, PAD, width)


def two_heads(q, k, v, mask, frames_scale):
    m = q.shape[0]
    n = k.shape[0]
    lane = lax.broadcasted_iota(jnp.int32, (m, 2 * HEAD_DIM), 1)
    first = lane < HEAD_DIM
    zero = jnp.zeros_like(q)
    stacked = jnp.concatenate([jnp.where(first, q, zero), jnp.where(first, zero, q)], axis=0)
    s = dot_t(stacked, k)
    if mask is not None:
        s = s + mask
    top = jnp.max(s, axis=-1, keepdims=True)
    p = jnp.exp2((s - top) * frames_scale).astype(BF16)
    both = dot(p, jnp.concatenate([v, jnp.ones((n, 2 * HEAD_DIM), BF16)], axis=1))
    d = 2 * HEAD_DIM
    num = jnp.where(first, both[:m, :d], both[m:, :d])
    den = jnp.where(first, both[:m, d:], both[m:, d:])
    return (num / den).astype(BF16)


def time_kernel(
    frames, part_ref, next_ref, w_ref, tgain_ref, wq_ref, wk_ref, wv_ref, wo_ref,
    xgain_ref, xq_ref, after_ref, query_ref, normed, tq, tk, tv, mixed, mask
):
    cols, slots, rows, _, width = part_ref.shape
    wide = 2 * width
    half = slots // 2
    total = cols * slots * rows * PAD
    block = half * rows * PAD
    side = 1 - first_row()
    other = next_ref[...].reshape(-1, wide)
    for c in range(2):
        after_ref[c] = part_ref[c]
        add = dot(other, w_ref[2 * side, pl.ds(1 - c, 2)].reshape(wide, width))
        after_ref[c, :, side * (rows - 1)] += add.reshape(slots, PAD, width)
    normed[...] = rms(after_ref[...].reshape(total, width), tgain_ref[...]).astype(BF16)
    tq[...] = dot(normed[...], wq_ref[...]).astype(BF16)
    tk[...] = dot(normed[...], wk_ref[...]).astype(BF16)
    tv[...] = dot(normed[...], wv_ref[...]).astype(BF16)
    row = lax.broadcasted_iota(jnp.int32, (2 * block, block), 0) % block
    col = lax.broadcasted_iota(jnp.int32, (2 * block, block), 1)
    mask[...] = jnp.where((row // PAD == col // PAD) & (col % PAD < frames), 0.0, NEG).astype(F32)
    for b in range(total // block):
        rs = slice(b * block, (b + 1) * block)
        for j in range(width // 128):
            ls = slice(j * 128, (j + 1) * 128)
            mixed[rs, ls] = two_heads(tq[rs, ls], tk[rs, ls], tv[rs, ls], mask[...], 0.125 * LOG2E)
    after_ref[...] += dot(mixed[...], wo_ref[...]).reshape(after_ref.shape)
    for c in range(2):
        nc = rms(after_ref[c, :half].reshape(block, width), xgain_ref[...]).astype(BF16)
        query_ref[c] = dot(nc, xq_ref[...]).astype(BF16).reshape(half, rows, PAD, width)


def cross_kernel(
    frames, slot_ref, gate_ref, after_ref, query_ref, own_ref, fetched_ref, swapped_ref, xo_ref, out_ref, mixed
):
    cols, slots, rows, _, width = after_ref.shape
    half = slots // 2
    even = first_row() == 1
    first_page = lax.axis_index("req") * REQ_DEV
    for r in range(half):
        page = slot_ref[first_page + r]
        i = lax.rem(page, REQ_DEV)
        mine = page - i == first_page
        k = jnp.where(mine, own_ref[0, i], jnp.where(even, fetched_ref[i], swapped_ref[i]))
        v = jnp.where(mine, own_ref[1, i], jnp.where(even, swapped_ref[i], fetched_ref[i]))
        q = query_ref[:, r].reshape(cols * rows * PAD, width)
        for j in range(width // 128):
            ls = slice(j * 128, (j + 1) * 128)
            out = two_heads(q[:, ls], k[:, ls], v[:, ls], None, 0.125 * LOG2E)
            mixed[:, r, :, :, ls] = out.reshape(cols, rows, PAD, 128)
    frame = lax.broadcasted_iota(jnp.int32, (rows, PAD, width), 1).astype(F32)
    scale = 1.0 + 2.0 * frame / (frames - 1)
    for c in range(cols):
        add = dot(mixed[c].reshape(-1, width), xo_ref[...]).reshape(half, rows, PAD, width)
        for r in range(half):
            cond = (after_ref[c, r] + add[r]).astype(BF16).astype(F32)
            uncond = after_ref[c, half + r].astype(BF16).astype(F32)
            guided = jnp.where(gate_ref[r] == 1, uncond + scale * (cond - uncond), cond)
            out_ref[r, :, :, c * width : (c + 1) * width] = guided.astype(BF16)


def on_device(
    hidden_states, gate, context_slot, context_pages, conv_weight, conv_bias, conv_gain, temporal_gain,
    temporal_query, temporal_key, temporal_value, temporal_out, cross_gain, cross_query, cross_out,
):
    _, _, rows, cols, frames, width = hidden_states.shape
    slots = 2 * REQ_DEV
    count = lax.axis_size("req")
    partner_pairs = [(i, i ^ (count // 2)) for i in range(count)]
    strips = lax.axis_size("strip")
    near_pairs, next_pairs = (
        [p for i in range(start, strips - 1, 2) for p in ((i, i + 1), (i + 1, i))] for start in (0, 1)
    )

    vm = pl.BlockSpec(memory_space=pltpu.VMEM)
    sm = pl.BlockSpec(memory_space=pltpu.SMEM)
    any_ = pl.BlockSpec(memory_space=pl.ANY)
    total = cols * slots * rows * PAD
    wide = cols * width
    raw = hidden_states.reshape((slots, rows, cols, frames, width)).transpose(0, 1, 3, 2, 4)
    stored = context_pages.transpose(0, 2, 1, 3)
    half = pl.pallas_call(
        pages_kernel,
        out_shape=jax.ShapeDtypeStruct(stored.shape[1:], BF16),
        in_specs=[any_],
        out_specs=vm,
        scratch_shapes=[pltpu.SemaphoreType.DMA],
        compiler_params=pltpu.CompilerParams(vmem_limit_bytes=8 << 20),
        cost_estimate=cost(COSTP),
        name="pages",
    )(stored)
    fetched = lax.ppermute(half, "req", partner_pairs)
    swapped = lax.ppermute(fetched, "strip", near_pairs)
    fetched = fetched.transpose(1, 0, 2)
    swapped = swapped.transpose(1, 0, 2)
    row = jax.ShapeDtypeStruct((slots, PAD, wide), BF16)
    whole = jax.ShapeDtypeStruct((slots, rows, PAD, wide), BF16)
    edge_x, edge_act = pl.pallas_call(
        edge_kernel,
        out_shape=(row, row),
        in_specs=[vm] * 2,
        out_specs=(vm, vm),
        compiler_params=pltpu.CompilerParams(vmem_limit_bytes=8 << 20),
        cost_estimate=cost(COST0),
        name="edge",
    )(raw, conv_gain)
    near = lax.ppermute(edge_act, "strip", near_pairs)
    x, act, edge = pl.pallas_call(
        act_kernel,
        out_shape=(whole, whole, row),
        in_specs=[vm] * 4,
        out_specs=(vm,) * 3,
        compiler_params=pltpu.CompilerParams(vmem_limit_bytes=8 << 20),
        cost_estimate=cost(COST1),
        name="activate",
    )(raw, conv_gain, edge_x, edge_act)
    other = lax.ppermute(edge, "strip", next_pairs)
    part = pl.pallas_call(
        conv_kernel,
        out_shape=jax.ShapeDtypeStruct((cols, slots, rows, PAD, width), F32),
        in_specs=[vm] * 5,
        out_specs=vm,
        scratch_shapes=[pltpu.VMEM((slots, rows + 2, PAD, wide), BF16)],
        compiler_params=pltpu.CompilerParams(vmem_limit_bytes=16 << 20),
        cost_estimate=cost(COST1),
        name="conv_own",
    )(x, act, near, conv_weight, conv_bias)
    after, query = pl.pallas_call(
        functools.partial(time_kernel, frames),
        out_shape=(
            jax.ShapeDtypeStruct((cols, slots, rows, PAD, width), F32),
            jax.ShapeDtypeStruct((cols, REQ_DEV, rows, PAD, width), BF16),
        ),
        in_specs=[vm] * 10,
        out_specs=(vm, vm),
        scratch_shapes=[pltpu.VMEM((total, width), BF16)] * 5
        + [
            pltpu.VMEM((slots * rows * PAD, slots * rows * PAD // 2), F32),
        ],
        compiler_params=pltpu.CompilerParams(vmem_limit_bytes=16 << 20),
        cost_estimate=cost(COST2),
        name="time_mix",
    )(
        part, other, conv_weight, temporal_gain, temporal_query, temporal_key,
        temporal_value, temporal_out, cross_gain, cross_query,
    )
    out = pl.pallas_call(
        functools.partial(cross_kernel, frames),
        out_shape=jax.ShapeDtypeStruct((REQ_DEV, rows, PAD, cols * width), BF16),
        in_specs=[sm, sm] + [vm] * 6,
        out_specs=vm,
        scratch_shapes=[pltpu.VMEM((cols, REQ_DEV, rows, PAD, width), BF16)],
        compiler_params=pltpu.CompilerParams(vmem_limit_bytes=8 << 20),
        cost_estimate=cost(COST3),
        name="cross_mix",
    )(context_slot, gate, after, query, context_pages, fetched, swapped, cross_out)
    out = out[:, :, :frames].reshape(REQ_DEV, rows, frames, cols, width)
    return out.transpose(0, 1, 3, 2, 4)


def solution(mesh):
    return jax.shard_map(
        on_device,
        mesh=mesh,
        in_specs=(
            P(None, "req", "strip", None, None, None),
            P("req"),
            P(),
            P(None, "req", None, None),
        )
        + (P(),) * 11,
        out_specs=P("req", "strip", None, None, None),
        check_vma=False,
    )
```

```python
import functools
import jax
import jax.numpy as jnp
from jax import lax
from jax.experimental import pallas as pl
from jax.experimental.pallas import tpu as pltpu
from jax.sharding import PartitionSpec as P

HEAD_DIM = 64
REQ_DEV = 2
PAD = 16
EPSILON = 1e-06
LOG2E = 1.4426950408889634
F32 = jnp.float32
BF16 = jnp.bfloat16
NEG = -1e30
COSTP, COST0, COST1, COST2, COST3 = 3 * 10**9, 16 * 10**9, 3 * 10**8, 6 * 10**9, 10**9


def cost(flops):
    return pl.CostEstimate(flops=flops, bytes_accessed=0, transcendentals=0)


def rms(x, gain):
    return x * lax.rsqrt(jnp.mean(x * x, axis=-1, keepdims=True) + EPSILON) * gain.reshape((1,) * (x.ndim - 1) + (-1,))


def silu(y):
    return y * (0.5 * jnp.tanh(0.5 * y) + 0.5)


def dot(a, b):
    return jnp.dot(a, b, preferred_element_type=F32)


def dot_t(a, b):
    return lax.dot_general(a, b, (((1,), (1,)), ((), ())), preferred_element_type=F32)


def pages_kernel(pages_ref, half_ref, sem):
    copy = pltpu.make_async_copy(pages_ref.at[1 - first_row()], half_ref, sem)
    copy.start()
    copy.wait()


def first_row():
    return 1 - lax.rem(lax.axis_index("strip"), 2)


def lay_out(raw_ref, gain_ref, s, r, c):
    frames, width = raw_ref.shape[2], raw_ref.shape[4]
    raw = raw_ref[s, r, :, c, :]
    raw = jnp.concatenate([raw, jnp.zeros((PAD - frames, width), BF16)], axis=0)
    return raw, silu(rms(raw.astype(F32), gain_ref[...])).astype(BF16)


def edge_kernel(raw_ref, gain_ref, x_ref, act_ref):
    slots, rows, _, cols, width = raw_ref.shape
    r = first_row() * (rows - 1)
    for s in range(slots):
        for c in range(cols):
            ls = slice(c * width, (c + 1) * width)
            x_ref[s, :, ls], act_ref[s, :, ls] = lay_out(raw_ref, gain_ref, s, r, c)


def act_kernel(raw_ref, gain_ref, edge_x_ref, edge_act_ref, x_ref, act_ref, edge_ref):
    slots, rows, _, cols, width = raw_ref.shape
    done = first_row() * (rows - 1)
    other = rows - 1 - done
    x_ref[:, done] = edge_x_ref[...]
    act_ref[:, done] = edge_act_ref[...]
    for s in range(slots):
        for c in range(cols):
            ls = slice(c * width, (c + 1) * width)
            for r in (other, *range(1, rows - 1)):
                x_ref[s, r, :, ls], a = lay_out(raw_ref, gain_ref, s, r, c)
                act_ref[s, r, :, ls] = a
                if r is other:
                    edge_ref[s, :, ls] = a


def conv_kernel(x_ref, act_ref, near_ref, w_ref, bias_ref, out_ref, ext):
    slots, rows, _, wide = x_ref.shape
    width = wide // 2
    side = 2 * first_row()
    ext[:, 1 : rows + 1] = act_ref[...]
    ext[:, side // 2 * (rows + 1)] = near_ref[...]
    both = jnp.concatenate(
        [ext[:, 1 : rows + 1].reshape(-1, wide), ext[:, pl.ds(side, rows)].reshape(-1, wide)], axis=-1
    )
    inner = ext[:, pl.ds(2 - side // 2, rows - 1)].reshape(-1, wide)
    inner_rows = pl.ds(side // 2, rows - 1)
    weights = jnp.concatenate([pair_taps(w_ref, 1), pair_taps(w_ref, side)], axis=0)
    mid = dot(both, weights)
    rest = dot(inner, pair_taps(w_ref, 2 - side))
    for c in range(2):
        ls = slice(c * width, (c + 1) * width)
        out_ref[c] = (
            x_ref[:, :, :, ls].astype(F32) + bias_ref[...].reshape(1, 1, 1, width) + mid[:, ls].reshape(slots, rows, PAD, width)
        )
        out_ref[c, :, inner_rows] += rest[:, ls].reshape(slots, rows - 1, PAD, width)


def pair_taps(w_ref, dr):
    wide = 2 * w_ref.shape[2]
    return jnp.concatenate([w_ref[dr, 1 - c : 3 - c].reshape(wide, wide // 2) for c in range(2)], axis=1)


def apart(x):
    first = lax.broadcasted_iota(jnp.int32, x.shape, 1) < HEAD_DIM
    zero = jnp.zeros_like(x)
    return jnp.concatenate([jnp.where(first, x, zero), jnp.where(first, zero, x)], axis=0)


def time_kernel(
    frames, part_ref, next_ref, w_ref, tgain_ref, wq_ref, wk_ref, wv_ref, wo_ref,
    xgain_ref, xq_ref, after_ref, query_ref, normed, tq, tk, tv, mixed, scores, chances
):
    cols, slots, rows, _, width = part_ref.shape
    wide = 2 * width
    half = slots // 2
    total = cols * slots * rows * PAD
    side = 1 - first_row()
    other = next_ref[...].reshape(-1, wide)
    add = dot(other, pair_taps(w_ref, 2 * side))
    for c in range(2):
        part_ref[c, :, side * (rows - 1)] += add[:, c * width : (c + 1) * width].reshape(slots, PAD, width)
    normed[...] = rms(part_ref[...].reshape(total, width), tgain_ref[...]).astype(BF16)
    every = dot(normed[...], jnp.concatenate([wq_ref[...], wk_ref[...], wv_ref[...]], axis=1))
    for i, part in enumerate((tq, tk, tv)):
        part[...] = every[:, i * width : (i + 1) * width].astype(BF16)
    group = rows * PAD
    pair = 2 * HEAD_DIM
    row = lax.broadcasted_iota(jnp.int32, (group, 2 * group), 0)
    col = lax.rem(lax.broadcasted_iota(jnp.int32, (group, 2 * group), 1), group)
    mask = jnp.where((row // PAD == col // PAD) & (lax.rem(col, PAD) < frames), 0.0, NEG).astype(F32)
    first = lax.broadcasted_iota(jnp.int32, (group, 2 * group), 1) < group
    ones = apart(jnp.ones((group, pair), BF16))
    tiles = [
        (slice(g * group, (g + 1) * group), slice(j * pair, (j + 1) * pair))
        for g in range(total // group)
        for j in range(width // pair)
    ]
    for rs, ls in tiles:
        scores[rs, ls] = dot_t(tq[rs, ls], apart(tk[rs, ls]))
    for rs, ls in tiles:
        s = scores[rs, ls] + mask
        top = jnp.where(
            first,
            jnp.max(jnp.where(first, s, NEG), axis=-1, keepdims=True),
            jnp.max(jnp.where(first, NEG, s), axis=-1, keepdims=True),
        )
        chances[rs, ls] = jnp.exp2((s - top) * (0.125 * LOG2E)).astype(BF16)
    for rs, ls in tiles:
        out = dot(chances[rs, ls], jnp.concatenate([apart(tv[rs, ls]), ones], axis=1))
        mixed[rs, ls] = (out[:, :pair] / out[:, pair:]).astype(BF16)
    after_ref[...] = part_ref[...] + dot(mixed[...], wo_ref[...]).reshape(after_ref.shape)
    nc = rms(after_ref[:, :half], xgain_ref[...]).astype(BF16).reshape(-1, width)
    query_ref[...] = dot(nc, xq_ref[...]).astype(BF16).reshape(query_ref.shape)


def cross_kernel(
    frames, slot_ref, gate_ref, after_ref, query_ref, own_ref, fetched_ref, swapped_ref, xo_ref, out_ref, keys, values, scores, chances, mixed
):
    cols, slots, rows, _, width = after_ref.shape
    half = slots // 2
    even = first_row() == 1
    tokens = own_ref.shape[2]
    room = -(-tokens // 128) * 128
    group = cols * rows * PAD
    pair = 2 * HEAD_DIM
    first_page = lax.axis_index("req") * REQ_DEV
    for r in range(half):
        page = slot_ref[first_page + r]
        i = lax.rem(page, REQ_DEV)
        mine = page - i == first_page
        k = jnp.where(mine, own_ref[0, i], jnp.where(even, fetched_ref[i], swapped_ref[i]))
        v = jnp.where(mine, own_ref[1, i], jnp.where(even, swapped_ref[i], fetched_ref[i]))
        tail = jnp.zeros((room - tokens, width), BF16)
        keys[r] = jnp.concatenate([k, tail], axis=0)
        values[r] = jnp.concatenate([v, tail], axis=0)
    tiles = [(r, slice(j * pair, (j + 1) * pair), slice(2 * j * room, 2 * (j + 1) * room)) for r in range(half) for j in range(width // pair)]
    live = lax.rem(lax.broadcasted_iota(jnp.int32, (group, 2 * room), 1), room) < tokens
    ones = apart(jnp.ones((room, pair), BF16))
    for r, ls, ks in tiles:
        scores[r, :, ks] = dot_t(query_ref[:, r, :, :, ls].reshape(group, pair), apart(keys[r, :, ls]))
    for r, ls, ks in tiles:
        s = jnp.where(live, scores[r, :, ks], NEG)
        p = [jnp.exp2((t - jnp.max(t, axis=-1, keepdims=True)) * (0.125 * LOG2E)) for t in (s[:, :room], s[:, room:])]
        chances[r, :, ks] = jnp.concatenate(p, axis=1).astype(BF16)
    for r, ls, ks in tiles:
        out = dot(chances[r, :, ks], jnp.concatenate([apart(values[r, :, ls]), ones], axis=1))
        mixed[:, r, :, :, ls] = (out[:, :pair] / out[:, pair:]).astype(BF16).reshape(cols, rows, PAD, pair)
    frame = lax.broadcasted_iota(jnp.int32, (rows, PAD, width), 1).astype(F32)
    scale = 1.0 + 2.0 * frame / (frames - 1)
    add = dot(mixed[...].reshape(-1, width), xo_ref[...]).reshape(cols, half, rows, PAD, width)
    for c in range(cols):
        for r in range(half):
            cond = (after_ref[c, r] + add[c, r]).astype(BF16).astype(F32)
            uncond = after_ref[c, half + r].astype(BF16).astype(F32)
            guided = jnp.where(gate_ref[r] == 1, uncond + scale * (cond - uncond), cond)
            out_ref[r, :, :, c * width : (c + 1) * width] = guided.astype(BF16)


def on_device(
    hidden_states, gate, context_slot, context_pages, conv_weight, conv_bias, conv_gain, temporal_gain,
    temporal_query, temporal_key, temporal_value, temporal_out, cross_gain, cross_query, cross_out,
):
    _, _, rows, cols, frames, width = hidden_states.shape
    slots = 2 * REQ_DEV
    count = lax.axis_size("req")
    partner_pairs = [(i, i ^ (count // 2)) for i in range(count)]
    strips = lax.axis_size("strip")
    near_pairs, next_pairs = (
        [p for i in range(start, strips - 1, 2) for p in ((i, i + 1), (i + 1, i))] for start in (0, 1)
    )

    vm = pl.BlockSpec(memory_space=pltpu.VMEM)
    sm = pl.BlockSpec(memory_space=pltpu.SMEM)
    any_ = pl.BlockSpec(memory_space=pl.ANY)
    total = cols * slots * rows * PAD
    wide = cols * width
    room = -(-context_pages.shape[2] // 128) * 128
    raw = hidden_states.reshape((slots, rows, cols, frames, width)).transpose(0, 1, 3, 2, 4)
    stored = context_pages.transpose(0, 2, 1, 3)
    half = pl.pallas_call(
        pages_kernel,
        out_shape=jax.ShapeDtypeStruct(stored.shape[1:], BF16),
        in_specs=[any_],
        out_specs=vm,
        scratch_shapes=[pltpu.SemaphoreType.DMA],
        compiler_params=pltpu.CompilerParams(vmem_limit_bytes=8 << 20),
        cost_estimate=cost(COSTP),
        name="pages",
    )(stored)
    fetched = lax.ppermute(half, "req", partner_pairs)
    swapped = lax.ppermute(fetched, "strip", near_pairs)
    fetched = fetched.transpose(1, 0, 2)
    swapped = swapped.transpose(1, 0, 2)
    row = jax.ShapeDtypeStruct((slots, PAD, wide), BF16)
    whole = jax.ShapeDtypeStruct((slots, rows, PAD, wide), BF16)
    edge_x, edge_act = pl.pallas_call(
        edge_kernel,
        out_shape=(row, row),
        in_specs=[vm] * 2,
        out_specs=(vm, vm),
        compiler_params=pltpu.CompilerParams(vmem_limit_bytes=8 << 20),
        cost_estimate=cost(COST0),
        name="edge",
    )(raw, conv_gain)
    near = lax.ppermute(edge_act, "strip", near_pairs)
    x, act, edge = pl.pallas_call(
        act_kernel,
        out_shape=(whole, whole, row),
        in_specs=[vm] * 4,
        out_specs=(vm,) * 3,
        compiler_params=pltpu.CompilerParams(vmem_limit_bytes=8 << 20),
        cost_estimate=cost(COST1),
        name="activate",
    )(raw, conv_gain, edge_x, edge_act)
    other = lax.ppermute(edge, "strip", next_pairs)
    part = pl.pallas_call(
        conv_kernel,
        out_shape=jax.ShapeDtypeStruct((cols, slots, rows, PAD, width), F32),
        in_specs=[vm] * 5,
        out_specs=vm,
        scratch_shapes=[pltpu.VMEM((slots, rows + 2, PAD, wide), BF16)],
        compiler_params=pltpu.CompilerParams(vmem_limit_bytes=16 << 20),
        cost_estimate=cost(COST1),
        name="conv_own",
    )(x, act, near, conv_weight, conv_bias)
    after, query = pl.pallas_call(
        functools.partial(time_kernel, frames),
        out_shape=(
            jax.ShapeDtypeStruct((cols, slots, rows, PAD, width), F32),
            jax.ShapeDtypeStruct((cols, REQ_DEV, rows, PAD, width), BF16),
        ),
        in_specs=[vm] * 10,
        out_specs=(vm, vm),
        scratch_shapes=[pltpu.VMEM((total, width), BF16)] * 5
        + [pltpu.VMEM((total, width // HEAD_DIM * rows * PAD), kind) for kind in (F32, BF16)],
        input_output_aliases={0: 0},
        compiler_params=pltpu.CompilerParams(vmem_limit_bytes=16 << 20),
        cost_estimate=cost(COST2),
        name="time_mix",
    )(
        part, other, conv_weight, temporal_gain, temporal_query, temporal_key,
        temporal_value, temporal_out, cross_gain, cross_query,
    )
    out = pl.pallas_call(
        functools.partial(cross_kernel, frames),
        out_shape=jax.ShapeDtypeStruct((REQ_DEV, rows, PAD, cols * width), BF16),
        in_specs=[sm, sm] + [vm] * 6,
        out_specs=vm,
        scratch_shapes=[pltpu.VMEM((REQ_DEV, room, width), BF16)] * 2
        + [
            pltpu.VMEM((REQ_DEV, cols * rows * PAD, width // HEAD_DIM * room), F32),
            pltpu.VMEM((REQ_DEV, cols * rows * PAD, width // HEAD_DIM * room), BF16),
            pltpu.VMEM((cols, REQ_DEV, rows, PAD, width), BF16),
        ],
        compiler_params=pltpu.CompilerParams(vmem_limit_bytes=16 << 20),
        cost_estimate=cost(COST3),
        name="cross_mix",
    )(context_slot, gate, after, query, context_pages, fetched, swapped, cross_out)
    out = out[:, :, :frames].reshape(REQ_DEV, rows, frames, cols, width)
    return out.transpose(0, 1, 3, 2, 4)


def solution(mesh):
    return jax.shard_map(
        on_device,
        mesh=mesh,
        in_specs=(
            P(None, "req", "strip", None, None, None),
            P("req"),
            P(),
            P(None, "req", None, None),
        )
        + (P(),) * 11,
        out_specs=P("req", "strip", None, None, None),
        check_vma=False,
    )
```

```python
import functools
import jax
import jax.numpy as jnp
from jax import lax
from jax.experimental import pallas as pl
from jax.experimental.pallas import tpu as pltpu
from jax.sharding import PartitionSpec as P

HEAD_DIM = 64
REQ_DEV = 2
PAD = 16
EPSILON = 1e-06
LOG2E = 1.4426950408889634
F32 = jnp.float32
BF16 = jnp.bfloat16
NEG = -1e30
COSTP, COST0, COST1, COST2, COST3 = 3 * 10**9, 16 * 10**9, 3 * 10**8, 6 * 10**9, 10**9


def cost(flops):
    return pl.CostEstimate(flops=flops, bytes_accessed=0, transcendentals=0)


def rms(x, gain):
    return x * lax.rsqrt(jnp.mean(x * x, axis=-1, keepdims=True) + EPSILON) * gain.reshape((1,) * (x.ndim - 1) + (-1,))


def silu(y):
    return y * (0.5 * jnp.tanh(0.5 * y) + 0.5)


def dot(a, b):
    return jnp.dot(a, b, preferred_element_type=F32)


def dot_t(a, b):
    return lax.dot_general(a, b, (((1,), (1,)), ((), ())), preferred_element_type=F32)


def pages_kernel(pages_ref, half_ref, sem):
    copy = pltpu.make_async_copy(pages_ref.at[1 - first_row()], half_ref, sem)
    copy.start()
    copy.wait()


def first_row():
    return 1 - lax.rem(lax.axis_index("strip"), 2)


def lay_out(raw_ref, gain_ref, s, r, x_ref, act_ref, *index):
    frames, cols, width = raw_ref.shape[2:]
    to = lax.broadcasted_iota(jnp.int32, (cols * PAD, cols * frames), 0)
    at = lax.broadcasted_iota(jnp.int32, (cols * PAD, cols * frames), 1)
    pick = (at == lax.rem(to, PAD) * cols + to // PAD) & (lax.rem(to, PAD) < frames)
    rows = dot(pick.astype(F32).astype(BF16), raw_ref[s, r].reshape(frames * cols, width))
    for c in range(cols):
        ls = slice(c * width, (c + 1) * width)
        one = rows[c * PAD : (c + 1) * PAD]
        x_ref[(*index, slice(None), ls)] = one.astype(BF16)
        act_ref[(*index, slice(None), ls)] = silu(rms(one, gain_ref[...])).astype(BF16)


def edge_kernel(raw_ref, gain_ref, x_ref, act_ref):
    slots, rows = raw_ref.shape[:2]
    r = first_row() * (rows - 1)
    for s in range(slots):
        lay_out(raw_ref, gain_ref, s, r, x_ref, act_ref, s)


def act_kernel(raw_ref, gain_ref, edge_x_ref, edge_act_ref, x_ref, act_ref, edge_ref):
    slots, rows = raw_ref.shape[:2]
    done = first_row() * (rows - 1)
    other = rows - 1 - done
    x_ref[:, done] = edge_x_ref[...]
    act_ref[:, done] = edge_act_ref[...]
    for s in range(slots):
        for r in (other, *range(1, rows - 1)):
            lay_out(raw_ref, gain_ref, s, r, x_ref, act_ref, s, r)
        edge_ref[s] = act_ref[s, other]


def conv_kernel(x_ref, act_ref, near_ref, w_ref, bias_ref, out_ref, ext):
    slots, rows, _, wide = x_ref.shape
    width = wide // 2
    side = 2 * first_row()
    ext[:, 1 : rows + 1] = act_ref[...]
    ext[:, side // 2 * (rows + 1)] = near_ref[...]
    both = jnp.concatenate(
        [ext[:, 1 : rows + 1].reshape(-1, wide), ext[:, pl.ds(side, rows)].reshape(-1, wide)], axis=-1
    )
    inner = ext[:, pl.ds(2 - side // 2, rows - 1)].reshape(-1, wide)
    inner_rows = pl.ds(side // 2, rows - 1)
    weights = jnp.concatenate([pair_taps(w_ref, 1), pair_taps(w_ref, side)], axis=0)
    mid = dot(both, weights)
    rest = dot(inner, pair_taps(w_ref, 2 - side))
    for c in range(2):
        ls = slice(c * width, (c + 1) * width)
        out_ref[c] = (
            x_ref[:, :, :, ls].astype(F32) + bias_ref[...].reshape(1, 1, 1, width) + mid[:, ls].reshape(slots, rows, PAD, width)
        )
        out_ref[c, :, inner_rows] += rest[:, ls].reshape(slots, rows - 1, PAD, width)


def pair_taps(w_ref, dr):
    wide = 2 * w_ref.shape[2]
    return jnp.concatenate([w_ref[dr, 1 - c : 3 - c].reshape(wide, wide // 2) for c in range(2)], axis=1)


def apart(x):
    first = lax.broadcasted_iota(jnp.int32, x.shape, 1) < HEAD_DIM
    zero = jnp.zeros_like(x)
    return jnp.concatenate([jnp.where(first, x, zero), jnp.where(first, zero, x)], axis=0)


def time_kernel(
    frames, part_ref, next_ref, w_ref, tgain_ref, wq_ref, wk_ref, wv_ref, wo_ref,
    xgain_ref, xq_ref, after_ref, query_ref, normed, tq, tk, tv, mixed, scores, chances
):
    cols, slots, rows, _, width = part_ref.shape
    wide = 2 * width
    half = slots // 2
    total = cols * slots * rows * PAD
    side = 1 - first_row()
    other = next_ref[...].reshape(-1, wide)
    add = dot(other, pair_taps(w_ref, 2 * side))
    for c in range(2):
        part_ref[c, :, side * (rows - 1)] += add[:, c * width : (c + 1) * width].reshape(slots, PAD, width)
    normed[...] = rms(part_ref[...].reshape(total, width), tgain_ref[...]).astype(BF16)
    every = dot(normed[...], jnp.concatenate([wq_ref[...], wk_ref[...], wv_ref[...]], axis=1))
    for i, part in enumerate((tq, tk, tv)):
        part[...] = every[:, i * width : (i + 1) * width].astype(BF16)
    group = rows * PAD
    pair = 2 * HEAD_DIM
    row = lax.broadcasted_iota(jnp.int32, (group, 2 * group), 0)
    col = lax.rem(lax.broadcasted_iota(jnp.int32, (group, 2 * group), 1), group)
    mask = jnp.where((row // PAD == col // PAD) & (lax.rem(col, PAD) < frames), 0.0, NEG).astype(F32)
    first = lax.broadcasted_iota(jnp.int32, (group, 2 * group), 1) < group
    ones = apart(jnp.ones((group, pair), BF16))
    tiles = [
        (slice(g * group, (g + 1) * group), slice(j * pair, (j + 1) * pair))
        for g in range(total // group)
        for j in range(width // pair)
    ]
    for rs, ls in tiles:
        scores[rs, ls] = dot_t(tq[rs, ls], apart(tk[rs, ls]))
    for rs, ls in tiles:
        s = scores[rs, ls] + mask
        top = jnp.where(
            first,
            jnp.max(jnp.where(first, s, NEG), axis=-1, keepdims=True),
            jnp.max(jnp.where(first, NEG, s), axis=-1, keepdims=True),
        )
        chances[rs, ls] = jnp.exp2((s - top) * (0.125 * LOG2E)).astype(BF16)
    for rs, ls in tiles:
        out = dot(chances[rs, ls], jnp.concatenate([apart(tv[rs, ls]), ones], axis=1))
        mixed[rs, ls] = (out[:, :pair] / out[:, pair:]).astype(BF16)
    after_ref[...] = part_ref[...] + dot(mixed[...], wo_ref[...]).reshape(after_ref.shape)
    nc = rms(after_ref[:, :half], xgain_ref[...]).astype(BF16).reshape(-1, width)
    query_ref[...] = dot(nc, xq_ref[...]).astype(BF16).reshape(query_ref.shape)


def cross_kernel(
    frames, slot_ref, gate_ref, after_ref, query_ref, own_ref, fetched_ref, swapped_ref, xo_ref, out_ref, keys, values, scores, chances, mixed, made, sems
):
    cols, slots, rows, _, width = after_ref.shape
    half = slots // 2
    even = first_row() == 1
    tokens = own_ref.shape[2]
    room = -(-tokens // 128) * 128
    group = cols * rows * PAD
    pair = 2 * HEAD_DIM
    first_page = lax.axis_index("req") * REQ_DEV
    for r in range(half):
        page = slot_ref[first_page + r]
        i = lax.rem(page, REQ_DEV)
        mine = page - i == first_page
        k = jnp.where(mine, own_ref[0, i], jnp.where(even, fetched_ref[i], swapped_ref[i]))
        v = jnp.where(mine, own_ref[1, i], jnp.where(even, swapped_ref[i], fetched_ref[i]))
        tail = jnp.zeros((room - tokens, width), BF16)
        keys[r] = jnp.concatenate([k, tail], axis=0)
        values[r] = jnp.concatenate([v, tail], axis=0)
    tiles = [(r, slice(j * pair, (j + 1) * pair), slice(2 * j * room, 2 * (j + 1) * room)) for r in range(half) for j in range(width // pair)]
    live = lax.rem(lax.broadcasted_iota(jnp.int32, (group, 2 * room), 1), room) < tokens
    ones = apart(jnp.ones((room, pair), BF16))
    for r, ls, ks in tiles:
        scores[r, :, ks] = dot_t(query_ref[:, r, :, :, ls].reshape(group, pair), apart(keys[r, :, ls]))
    for r, ls, ks in tiles:
        s = jnp.where(live, scores[r, :, ks], NEG)
        p = [jnp.exp2((t - jnp.max(t, axis=-1, keepdims=True)) * (0.125 * LOG2E)) for t in (s[:, :room], s[:, room:])]
        chances[r, :, ks] = jnp.concatenate(p, axis=1).astype(BF16)
    for r, ls, ks in tiles:
        out = dot(chances[r, :, ks], jnp.concatenate([apart(values[r, :, ls]), ones], axis=1))
        mixed[:, r, :, :, ls] = (out[:, :pair] / out[:, pair:]).astype(BF16).reshape(cols, rows, PAD, pair)
    frame = lax.broadcasted_iota(jnp.int32, (rows, PAD, width), 1).astype(F32)
    scale = 1.0 + 2.0 * frame / (frames - 1)
    add = dot(mixed[...].reshape(-1, width), xo_ref[...]).reshape(cols, half, rows, PAD, width)
    copies = []
    for r in range(half):
        for c in range(cols):
            cond = (after_ref[c, r] + add[c, r]).astype(BF16).astype(F32)
            uncond = after_ref[c, half + r].astype(BF16).astype(F32)
            guided = jnp.where(gate_ref[r] == 1, uncond + scale * (cond - uncond), cond)
            for w in range(rows):
                made[r, w, :, c, :] = guided[w, :frames].astype(BF16)
        copies.append(pltpu.make_async_copy(made.at[r], out_ref.at[r], sems.at[r]))
        copies[r].start()
    for copy in copies:
        copy.wait()


def on_device(
    hidden_states, gate, context_slot, context_pages, conv_weight, conv_bias, conv_gain, temporal_gain,
    temporal_query, temporal_key, temporal_value, temporal_out, cross_gain, cross_query, cross_out,
):
    _, _, rows, cols, frames, width = hidden_states.shape
    slots = 2 * REQ_DEV
    count = lax.axis_size("req")
    partner_pairs = [(i, i ^ (count // 2)) for i in range(count)]
    strips = lax.axis_size("strip")
    near_pairs, next_pairs = (
        [p for i in range(start, strips - 1, 2) for p in ((i, i + 1), (i + 1, i))] for start in (0, 1)
    )

    vm = pl.BlockSpec(memory_space=pltpu.VMEM)
    sm = pl.BlockSpec(memory_space=pltpu.SMEM)
    any_ = pl.BlockSpec(memory_space=pl.ANY)
    total = cols * slots * rows * PAD
    wide = cols * width
    room = -(-context_pages.shape[2] // 128) * 128
    raw = hidden_states.reshape((slots, rows, cols, frames, width)).transpose(0, 1, 3, 2, 4)
    stored = context_pages.transpose(0, 2, 1, 3)
    half = pl.pallas_call(
        pages_kernel,
        out_shape=jax.ShapeDtypeStruct(stored.shape[1:], BF16),
        in_specs=[any_],
        out_specs=vm,
        scratch_shapes=[pltpu.SemaphoreType.DMA],
        compiler_params=pltpu.CompilerParams(vmem_limit_bytes=8 << 20),
        cost_estimate=cost(COSTP),
        name="pages",
    )(stored)
    fetched = lax.ppermute(half, "req", partner_pairs)
    swapped = lax.ppermute(fetched, "strip", near_pairs)
    fetched = fetched.transpose(1, 0, 2)
    swapped = swapped.transpose(1, 0, 2)
    row = jax.ShapeDtypeStruct((slots, PAD, wide), BF16)
    whole = jax.ShapeDtypeStruct((slots, rows, PAD, wide), BF16)
    edge_x, edge_act = pl.pallas_call(
        edge_kernel,
        out_shape=(row, row),
        in_specs=[vm] * 2,
        out_specs=(vm, vm),
        compiler_params=pltpu.CompilerParams(vmem_limit_bytes=8 << 20),
        cost_estimate=cost(COST0),
        name="edge",
    )(raw, conv_gain)
    near = lax.ppermute(edge_act, "strip", near_pairs)
    x, act, edge = pl.pallas_call(
        act_kernel,
        out_shape=(whole, whole, row),
        in_specs=[vm] * 4,
        out_specs=(vm,) * 3,
        compiler_params=pltpu.CompilerParams(vmem_limit_bytes=8 << 20),
        cost_estimate=cost(COST1),
        name="activate",
    )(raw, conv_gain, edge_x, edge_act)
    other = lax.ppermute(edge, "strip", next_pairs)
    part = pl.pallas_call(
        conv_kernel,
        out_shape=jax.ShapeDtypeStruct((cols, slots, rows, PAD, width), F32),
        in_specs=[vm] * 5,
        out_specs=vm,
        scratch_shapes=[pltpu.VMEM((slots, rows + 2, PAD, wide), BF16)],
        compiler_params=pltpu.CompilerParams(vmem_limit_bytes=16 << 20),
        cost_estimate=cost(COST1),
        name="conv_own",
    )(x, act, near, conv_weight, conv_bias)
    after, query = pl.pallas_call(
        functools.partial(time_kernel, frames),
        out_shape=(
            jax.ShapeDtypeStruct((cols, slots, rows, PAD, width), F32),
            jax.ShapeDtypeStruct((cols, REQ_DEV, rows, PAD, width), BF16),
        ),
        in_specs=[vm] * 10,
        out_specs=(vm, vm),
        scratch_shapes=[pltpu.VMEM((total, width), BF16)] * 5
        + [pltpu.VMEM((total, width // HEAD_DIM * rows * PAD), kind) for kind in (F32, BF16)],
        input_output_aliases={0: 0},
        compiler_params=pltpu.CompilerParams(vmem_limit_bytes=16 << 20),
        cost_estimate=cost(COST2),
        name="time_mix",
    )(
        part, other, conv_weight, temporal_gain, temporal_query, temporal_key,
        temporal_value, temporal_out, cross_gain, cross_query,
    )
    out = pl.pallas_call(
        functools.partial(cross_kernel, frames),
        out_shape=jax.ShapeDtypeStruct((REQ_DEV, rows, frames, cols, width), BF16),
        in_specs=[sm, sm] + [vm] * 6,
        out_specs=any_,
        scratch_shapes=[pltpu.VMEM((REQ_DEV, room, width), BF16)] * 2
        + [
            pltpu.VMEM((REQ_DEV, cols * rows * PAD, width // HEAD_DIM * room), F32),
            pltpu.VMEM((REQ_DEV, cols * rows * PAD, width // HEAD_DIM * room), BF16),
            pltpu.VMEM((cols, REQ_DEV, rows, PAD, width), BF16),
            pltpu.VMEM((REQ_DEV, rows, frames, cols, width), BF16),
            pltpu.SemaphoreType.DMA((REQ_DEV,)),
        ],
        compiler_params=pltpu.CompilerParams(vmem_limit_bytes=16 << 20),
        cost_estimate=cost(COST3),
        name="cross_mix",
    )(context_slot, gate, after, query, context_pages, fetched, swapped, cross_out)
    return out.transpose(0, 1, 3, 2, 4)


def solution(mesh):
    return jax.shard_map(
        on_device,
        mesh=mesh,
        in_specs=(
            P(None, "req", "strip", None, None, None),
            P("req"),
            P(),
            P(None, "req", None, None),
        )
        + (P(),) * 11,
        out_specs=P("req", "strip", None, None, None),
        check_vma=False,
    )
```

```python
import functools
import jax
import jax.numpy as jnp
from jax import lax
from jax.experimental import pallas as pl
from jax.experimental.pallas import tpu as pltpu
from jax.sharding import PartitionSpec as P

HEAD_DIM = 64
REQ_DEV = 2
PAD = 16
EPSILON = 1e-06
LOG2E = 1.4426950408889634
F32 = jnp.float32
BF16 = jnp.bfloat16
NEG = -1e30
COSTP, COST0, COST1, COST2, COST3 = 3 * 10**9, 16 * 10**9, 3 * 10**8, 6 * 10**9, 10**9


def cost(flops):
    return pl.CostEstimate(flops=flops, bytes_accessed=0, transcendentals=0)


def rms(x, gain):
    return x * lax.rsqrt(jnp.mean(x * x, axis=-1, keepdims=True) + EPSILON) * gain.reshape((1,) * (x.ndim - 1) + (-1,))


def silu(y):
    return y * (0.5 * jnp.tanh(0.5 * y) + 0.5)


def dot(a, b):
    return jnp.dot(a, b, preferred_element_type=F32)


def dot_t(a, b):
    return lax.dot_general(a, b, (((1,), (1,)), ((), ())), preferred_element_type=F32)


def pages_kernel(pages_ref, half_ref, sem):
    copy = pltpu.make_async_copy(pages_ref.at[1 - first_row()], half_ref, sem)
    copy.start()
    copy.wait()


def first_row():
    return 1 - lax.rem(lax.axis_index("strip"), 2)


def lay_out(raw_ref, gain_ref, s, r, x_ref, act_ref, *index):
    frames, cols, width = raw_ref.shape[2:]
    to = lax.broadcasted_iota(jnp.int32, (cols * PAD, cols * frames), 0)
    at = lax.broadcasted_iota(jnp.int32, (cols * PAD, cols * frames), 1)
    pick = (at == lax.rem(to, PAD) * cols + to // PAD) & (lax.rem(to, PAD) < frames)
    rows = dot(pick.astype(F32).astype(BF16), raw_ref[s, r].reshape(frames * cols, width))
    for c in range(cols):
        ls = slice(c * width, (c + 1) * width)
        one = rows[c * PAD : (c + 1) * PAD]
        x_ref[(*index, slice(None), ls)] = one.astype(BF16)
        act_ref[(*index, slice(None), ls)] = silu(rms(one, gain_ref[...])).astype(BF16)


def edge_kernel(raw_ref, gain_ref, x_ref, act_ref):
    slots, rows = raw_ref.shape[:2]
    r = first_row() * (rows - 1)
    for s in range(slots):
        lay_out(raw_ref, gain_ref, s, r, x_ref, act_ref, s)


def act_kernel(raw_ref, gain_ref, edge_x_ref, edge_act_ref, x_ref, act_ref, edge_ref):
    slots, rows = raw_ref.shape[:2]
    done = first_row() * (rows - 1)
    other = rows - 1 - done
    x_ref[:, done] = edge_x_ref[...]
    act_ref[:, done] = edge_act_ref[...]
    for s in range(slots):
        for r in (other, *range(1, rows - 1)):
            lay_out(raw_ref, gain_ref, s, r, x_ref, act_ref, s, r)
        edge_ref[s] = act_ref[s, other]


def conv_kernel(
    x_ref, act_ref, near_ref, w_ref, bias_ref, tgain_ref, wq_ref, out_ref, normed_ref, tq_ref, ext
):
    slots, rows, _, wide = x_ref.shape
    width = wide // 2
    side = 2 * first_row()
    ext[:, 1 : rows + 1] = act_ref[...]
    ext[:, side // 2 * (rows + 1)] = near_ref[...]
    both = jnp.concatenate(
        [ext[:, 1 : rows + 1].reshape(-1, wide), ext[:, pl.ds(side, rows)].reshape(-1, wide)], axis=-1
    )
    inner = ext[:, pl.ds(2 - side // 2, rows - 1)].reshape(-1, wide)
    inner_rows = pl.ds(side // 2, rows - 1)
    weights = jnp.concatenate([pair_taps(w_ref, 1), pair_taps(w_ref, side)], axis=0)
    mid = dot(both, weights)
    rest = dot(inner, pair_taps(w_ref, 2 - side))
    for c in range(2):
        ls = slice(c * width, (c + 1) * width)
        out_ref[c] = (
            x_ref[:, :, :, ls].astype(F32) + bias_ref[...].reshape(1, 1, 1, width) + mid[:, ls].reshape(slots, rows, PAD, width)
        )
        out_ref[c, :, inner_rows] += rest[:, ls].reshape(slots, rows - 1, PAD, width)
    normalize(out_ref, tgain_ref, wq_ref, normed_ref, tq_ref, pl.ds(side // 2, rows - 1))


def normalize(field_ref, gain_ref, wq_ref, normed_ref, tq_ref, place):
    field = rms(field_ref[:, :, place], gain_ref[...]).astype(BF16)
    normed_ref[:, :, place] = field
    tq_ref[:, :, place] = dot(field.reshape(-1, field.shape[-1]), wq_ref[...]).astype(BF16).reshape(field.shape)


def pair_taps(w_ref, dr):
    wide = 2 * w_ref.shape[2]
    return jnp.concatenate([w_ref[dr, 1 - c : 3 - c].reshape(wide, wide // 2) for c in range(2)], axis=1)


def apart(x):
    first = lax.broadcasted_iota(jnp.int32, x.shape, 1) < HEAD_DIM
    zero = jnp.zeros_like(x)
    return jnp.concatenate([jnp.where(first, x, zero), jnp.where(first, zero, x)], axis=0)


def time_kernel(
    frames, part_ref, normed, tq, next_ref, w_ref, tgain_ref, wq_ref, wk_ref, wv_ref, wo_ref,
    xgain_ref, xq_ref, after_ref, _normed, _tq, query_ref, tk, tv, mixed, scores, chances
):
    cols, slots, rows, _, width = part_ref.shape
    wide = 2 * width
    half = slots // 2
    total = cols * slots * rows * PAD
    side = 1 - first_row()
    other = next_ref[...].reshape(-1, wide)
    add = dot(other, pair_taps(w_ref, 2 * side))
    for c in range(2):
        part_ref[c, :, side * (rows - 1)] += add[:, c * width : (c + 1) * width].reshape(slots, PAD, width)
    normalize(part_ref, tgain_ref, wq_ref, normed, tq, pl.ds(side * (rows - 1), 1))
    both = dot(normed[...].reshape(total, width), jnp.concatenate([wk_ref[...], wv_ref[...]], axis=1))
    tk[...] = both[:, :width].astype(BF16)
    tv[...] = both[:, width:].astype(BF16)
    group = rows * PAD
    pair = 2 * HEAD_DIM
    row = lax.broadcasted_iota(jnp.int32, (group, 2 * group), 0)
    col = lax.rem(lax.broadcasted_iota(jnp.int32, (group, 2 * group), 1), group)
    mask = jnp.where((row // PAD == col // PAD) & (lax.rem(col, PAD) < frames), 0.0, NEG).astype(F32)
    first = lax.broadcasted_iota(jnp.int32, (group, 2 * group), 1) < group
    ones = apart(jnp.ones((group, pair), BF16))
    tiles = [
        (g, slice(g * group, (g + 1) * group), slice(j * pair, (j + 1) * pair))
        for g in range(total // group)
        for j in range(width // pair)
    ]
    for g, rs, ls in tiles:
        query = tq[g // slots, g % slots, :, :, ls].reshape(group, pair)
        scores[rs, ls] = dot_t(query, apart(tk[rs, ls]))
    for _, rs, ls in tiles:
        s = scores[rs, ls] + mask
        top = jnp.where(
            first,
            jnp.max(jnp.where(first, s, NEG), axis=-1, keepdims=True),
            jnp.max(jnp.where(first, NEG, s), axis=-1, keepdims=True),
        )
        chances[rs, ls] = jnp.exp2((s - top) * (0.125 * LOG2E)).astype(BF16)
    for _, rs, ls in tiles:
        out = dot(chances[rs, ls], jnp.concatenate([apart(tv[rs, ls]), ones], axis=1))
        mixed[rs, ls] = (out[:, :pair] / out[:, pair:]).astype(BF16)
    after_ref[...] = part_ref[...] + dot(mixed[...], wo_ref[...]).reshape(after_ref.shape)
    nc = rms(after_ref[:, :half], xgain_ref[...]).astype(BF16).reshape(-1, width)
    query_ref[...] = dot(nc, xq_ref[...]).astype(BF16).reshape(query_ref.shape)


def cross_kernel(
    frames, slot_ref, gate_ref, after_ref, query_ref, own_ref, fetched_ref, swapped_ref, xo_ref, out_ref, keys, values, scores, chances, mixed, made, sems
):
    cols, slots, rows, _, width = after_ref.shape
    half = slots // 2
    even = first_row() == 1
    tokens = own_ref.shape[2]
    room = -(-tokens // 128) * 128
    group = cols * rows * PAD
    pair = 2 * HEAD_DIM
    first_page = lax.axis_index("req") * REQ_DEV
    for r in range(half):
        page = slot_ref[first_page + r]
        i = lax.rem(page, REQ_DEV)
        mine = page - i == first_page
        k = jnp.where(mine, own_ref[0, i], jnp.where(even, fetched_ref[i], swapped_ref[i]))
        v = jnp.where(mine, own_ref[1, i], jnp.where(even, swapped_ref[i], fetched_ref[i]))
        tail = jnp.zeros((room - tokens, width), BF16)
        keys[r] = jnp.concatenate([k, tail], axis=0)
        values[r] = jnp.concatenate([v, tail], axis=0)
    tiles = [(r, slice(j * pair, (j + 1) * pair), slice(2 * j * room, 2 * (j + 1) * room)) for r in range(half) for j in range(width // pair)]
    live = lax.rem(lax.broadcasted_iota(jnp.int32, (group, 2 * room), 1), room) < tokens
    ones = apart(jnp.ones((room, pair), BF16))
    for r, ls, ks in tiles:
        scores[r, :, ks] = dot_t(query_ref[:, r, :, :, ls].reshape(group, pair), apart(keys[r, :, ls]))
    for r, ls, ks in tiles:
        s = jnp.where(live, scores[r, :, ks], NEG)
        p = [jnp.exp2((t - jnp.max(t, axis=-1, keepdims=True)) * (0.125 * LOG2E)) for t in (s[:, :room], s[:, room:])]
        chances[r, :, ks] = jnp.concatenate(p, axis=1).astype(BF16)
    for r, ls, ks in tiles:
        out = dot(chances[r, :, ks], jnp.concatenate([apart(values[r, :, ls]), ones], axis=1))
        mixed[:, r, :, :, ls] = (out[:, :pair] / out[:, pair:]).astype(BF16).reshape(cols, rows, PAD, pair)
    frame = lax.broadcasted_iota(jnp.int32, (PAD, width), 0).astype(F32)
    scale = 1.0 + 2.0 * frame / (frames - 1)
    add = dot(mixed[...].reshape(-1, width), xo_ref[...]).reshape(cols, half, rows, PAD, width)
    copies = []
    for r in range(half):
        for c in range(cols):
            cond = (after_ref[c, r] + add[c, r]).astype(BF16).astype(F32)
            uncond = after_ref[c, half + r].astype(BF16).astype(F32)
            guided = jnp.where(gate_ref[r] == 1, uncond + scale * (cond - uncond), cond)
            for w in range(rows):
                made[r, w, :, c, :] = guided[w, :frames].astype(BF16)
        copies.append(pltpu.make_async_copy(made.at[r], out_ref.at[r], sems.at[r]))
        copies[r].start()
    for copy in copies:
        copy.wait()


def on_device(
    hidden_states, gate, context_slot, context_pages, conv_weight, conv_bias, conv_gain, temporal_gain,
    temporal_query, temporal_key, temporal_value, temporal_out, cross_gain, cross_query, cross_out,
):
    _, _, rows, cols, frames, width = hidden_states.shape
    slots = 2 * REQ_DEV
    count = lax.axis_size("req")
    partner_pairs = [(i, i ^ (count // 2)) for i in range(count)]
    strips = lax.axis_size("strip")
    near_pairs, next_pairs = (
        [p for i in range(start, strips - 1, 2) for p in ((i, i + 1), (i + 1, i))] for start in (0, 1)
    )

    vm = pl.BlockSpec(memory_space=pltpu.VMEM)
    sm = pl.BlockSpec(memory_space=pltpu.SMEM)
    any_ = pl.BlockSpec(memory_space=pl.ANY)
    total = cols * slots * rows * PAD
    wide = cols * width
    room = -(-context_pages.shape[2] // 128) * 128
    raw = hidden_states.reshape((slots, rows, cols, frames, width)).transpose(0, 1, 3, 2, 4)
    stored = context_pages.transpose(0, 2, 1, 3)
    half = pl.pallas_call(
        pages_kernel,
        out_shape=jax.ShapeDtypeStruct(stored.shape[1:], BF16),
        in_specs=[any_],
        out_specs=vm,
        scratch_shapes=[pltpu.SemaphoreType.DMA],
        compiler_params=pltpu.CompilerParams(vmem_limit_bytes=8 << 20),
        cost_estimate=cost(COSTP),
        name="pages",
    )(stored)
    fetched = lax.ppermute(half, "req", partner_pairs)
    swapped = lax.ppermute(fetched, "strip", near_pairs)
    fetched = fetched.transpose(1, 0, 2)
    swapped = swapped.transpose(1, 0, 2)
    row = jax.ShapeDtypeStruct((slots, PAD, wide), BF16)
    whole = jax.ShapeDtypeStruct((slots, rows, PAD, wide), BF16)
    edge_x, edge_act = pl.pallas_call(
        edge_kernel,
        out_shape=(row, row),
        in_specs=[vm] * 2,
        out_specs=(vm, vm),
        compiler_params=pltpu.CompilerParams(vmem_limit_bytes=8 << 20),
        cost_estimate=cost(COST0),
        name="edge",
    )(raw, conv_gain)
    near = lax.ppermute(edge_act, "strip", near_pairs)
    x, act, edge = pl.pallas_call(
        act_kernel,
        out_shape=(whole, whole, row),
        in_specs=[vm] * 4,
        out_specs=(vm,) * 3,
        compiler_params=pltpu.CompilerParams(vmem_limit_bytes=8 << 20),
        cost_estimate=cost(COST1),
        name="activate",
    )(raw, conv_gain, edge_x, edge_act)
    other = lax.ppermute(edge, "strip", next_pairs)
    grid = (cols, slots, rows, PAD, width)
    part, normed, queries = pl.pallas_call(
        conv_kernel,
        out_shape=(jax.ShapeDtypeStruct(grid, F32), jax.ShapeDtypeStruct(grid, BF16), jax.ShapeDtypeStruct(grid, BF16)),
        in_specs=[vm] * 7,
        out_specs=(vm,) * 3,
        scratch_shapes=[pltpu.VMEM((slots, rows + 2, PAD, wide), BF16)],
        compiler_params=pltpu.CompilerParams(vmem_limit_bytes=16 << 20),
        cost_estimate=cost(COST1),
        name="conv_own",
    )(x, act, near, conv_weight, conv_bias, temporal_gain, temporal_query)
    after, _, _, query = pl.pallas_call(
        functools.partial(time_kernel, frames),
        out_shape=(
            jax.ShapeDtypeStruct(grid, F32),
            jax.ShapeDtypeStruct(grid, BF16),
            jax.ShapeDtypeStruct(grid, BF16),
            jax.ShapeDtypeStruct((cols, REQ_DEV, rows, PAD, width), BF16),
        ),
        in_specs=[vm] * 12,
        out_specs=(vm,) * 4,
        scratch_shapes=[pltpu.VMEM((total, width), BF16)] * 3
        + [pltpu.VMEM((total, width // HEAD_DIM * rows * PAD), kind) for kind in (F32, BF16)],
        input_output_aliases={0: 0, 1: 1, 2: 2},
        compiler_params=pltpu.CompilerParams(vmem_limit_bytes=16 << 20),
        cost_estimate=cost(COST2),
        name="time_mix",
    )(
        part, normed, queries, other, conv_weight, temporal_gain, temporal_query, temporal_key, temporal_value,
        temporal_out, cross_gain, cross_query,
    )
    out = pl.pallas_call(
        functools.partial(cross_kernel, frames),
        out_shape=jax.ShapeDtypeStruct((REQ_DEV, rows, frames, cols, width), BF16),
        in_specs=[sm, sm] + [vm] * 6,
        out_specs=any_,
        scratch_shapes=[pltpu.VMEM((REQ_DEV, room, width), BF16)] * 2
        + [
            pltpu.VMEM((REQ_DEV, cols * rows * PAD, width // HEAD_DIM * room), F32),
            pltpu.VMEM((REQ_DEV, cols * rows * PAD, width // HEAD_DIM * room), BF16),
            pltpu.VMEM((cols, REQ_DEV, rows, PAD, width), BF16),
            pltpu.VMEM((REQ_DEV, rows, frames, cols, width), BF16),
            pltpu.SemaphoreType.DMA((REQ_DEV,)),
        ],
        compiler_params=pltpu.CompilerParams(vmem_limit_bytes=16 << 20),
        cost_estimate=cost(COST3),
        name="cross_mix",
    )(context_slot, gate, after, query, context_pages, fetched, swapped, cross_out)
    return out.transpose(0, 1, 3, 2, 4)


def solution(mesh):
    return jax.shard_map(
        on_device,
        mesh=mesh,
        in_specs=(
            P(None, "req", "strip", None, None, None),
            P("req"),
            P(),
            P(None, "req", None, None),
        )
        + (P(),) * 11,
        out_specs=P("req", "strip", None, None, None),
        check_vma=False,
    )
```

```python
import functools
import jax
import jax.numpy as jnp
from jax import lax
from jax.experimental import pallas as pl
from jax.experimental.pallas import tpu as pltpu
from jax.sharding import PartitionSpec as P

HEAD_DIM = 64
REQ_DEV = 2
PAD = 16
EPSILON = 1e-06
LOG2E = 1.4426950408889634
F32 = jnp.float32
BF16 = jnp.bfloat16
NEG = -1e30
COSTP, COST0, COST1, COST2, COST3 = 3 * 10**9, 16 * 10**9, 3 * 10**8, 6 * 10**9, 10**9


def cost(flops):
    return pl.CostEstimate(flops=flops, bytes_accessed=0, transcendentals=0)


def rms(x, gain):
    return x * lax.rsqrt(jnp.mean(x * x, axis=-1, keepdims=True) + EPSILON) * gain.reshape((1,) * (x.ndim - 1) + (-1,))


def silu(y):
    return y * (0.5 * jnp.tanh(0.5 * y) + 0.5)


def dot(a, b):
    return jnp.dot(a, b, preferred_element_type=F32)


def dot_t(a, b):
    return lax.dot_general(a, b, (((1,), (1,)), ((), ())), preferred_element_type=F32)


def pages_kernel(pages_ref, half_ref, sem):
    copy = pltpu.make_async_copy(pages_ref.at[1 - first_row()], half_ref, sem)
    copy.start()
    copy.wait()


def first_row():
    return 1 - lax.rem(lax.axis_index("strip"), 2)


def lay_out(raw_ref, gain_ref, s, r, x_ref, act_ref, *index):
    frames, cols, width = raw_ref.shape[2:]
    to = lax.broadcasted_iota(jnp.int32, (cols * PAD, cols * frames), 0)
    at = lax.broadcasted_iota(jnp.int32, (cols * PAD, cols * frames), 1)
    pick = (at == lax.rem(to, PAD) * cols + to // PAD) & (lax.rem(to, PAD) < frames)
    rows = dot(pick.astype(F32).astype(BF16), raw_ref[s, r].reshape(frames * cols, width))
    for c in range(cols):
        ls = slice(c * width, (c + 1) * width)
        one = rows[c * PAD : (c + 1) * PAD]
        x_ref[(*index, slice(None), ls)] = one.astype(BF16)
        act_ref[(*index, slice(None), ls)] = silu(rms(one, gain_ref[...])).astype(BF16)


def edge_kernel(raw_ref, gain_ref, x_ref, act_ref):
    slots, rows = raw_ref.shape[:2]
    r = first_row() * (rows - 1)
    for s in range(slots):
        lay_out(raw_ref, gain_ref, s, r, x_ref, act_ref, s)


def act_kernel(raw_ref, gain_ref, edge_x_ref, edge_act_ref, x_ref, act_ref, edge_ref):
    slots, rows = raw_ref.shape[:2]
    done = first_row() * (rows - 1)
    other = rows - 1 - done
    x_ref[:, done] = edge_x_ref[...]
    act_ref[:, done] = edge_act_ref[...]
    for s in range(slots):
        for r in (other, *range(1, rows - 1)):
            lay_out(raw_ref, gain_ref, s, r, x_ref, act_ref, s, r)
        edge_ref[s] = act_ref[s, other]


def conv_kernel(
    x_ref, act_ref, near_ref, w_ref, bias_ref, tgain_ref, wq_ref, out_ref, normed_ref, tq_ref, ext
):
    slots, rows, _, wide = x_ref.shape
    width = wide // 2
    side = 2 * first_row()
    ext[:, 1 : rows + 1] = act_ref[...]
    ext[:, side // 2 * (rows + 1)] = near_ref[...]
    both = jnp.concatenate(
        [ext[:, 1 : rows + 1].reshape(-1, wide), ext[:, pl.ds(side, rows)].reshape(-1, wide)], axis=-1
    )
    inner = ext[:, pl.ds(2 - side // 2, rows - 1)].reshape(-1, wide)
    inner_rows = pl.ds(side // 2, rows - 1)
    weights = jnp.concatenate([pair_taps(w_ref, 1), pair_taps(w_ref, side)], axis=0)
    mid = dot(both, weights)
    rest = dot(inner, pair_taps(w_ref, 2 - side))
    for c in range(2):
        ls = slice(c * width, (c + 1) * width)
        out_ref[c] = (
            x_ref[:, :, :, ls].astype(F32) + bias_ref[...].reshape(1, 1, 1, width) + mid[:, ls].reshape(slots, rows, PAD, width)
        )
        out_ref[c, :, inner_rows] += rest[:, ls].reshape(slots, rows - 1, PAD, width)
    normalize(out_ref, tgain_ref, wq_ref, normed_ref, tq_ref, pl.ds(side // 2, rows - 1))


def normalize(field_ref, gain_ref, wq_ref, normed_ref, tq_ref, place):
    field = rms(field_ref[:, :, place], gain_ref[...]).astype(BF16)
    normed_ref[:, :, place] = field
    tq_ref[:, :, place] = dot(field.reshape(-1, field.shape[-1]), wq_ref[...]).astype(BF16).reshape(field.shape)


def pair_taps(w_ref, dr):
    wide = 2 * w_ref.shape[2]
    return jnp.concatenate([w_ref[dr, 1 - c : 3 - c].reshape(wide, wide // 2) for c in range(2)], axis=1)


def apart(x):
    first = lax.broadcasted_iota(jnp.int32, x.shape, 1) < HEAD_DIM
    zero = jnp.zeros_like(x)
    return jnp.concatenate([jnp.where(first, x, zero), jnp.where(first, zero, x)], axis=0)


def time_kernel(
    frames, part_ref, normed, tq, next_ref, w_ref, tgain_ref, wq_ref, wk_ref, wv_ref, wo_ref,
    xgain_ref, xq_ref, after_ref, _normed, _tq, query_ref, tk, tv, mixed, scores, chances
):
    cols, slots, rows, _, width = part_ref.shape
    wide = 2 * width
    half = slots // 2
    total = cols * slots * rows * PAD
    side = 1 - first_row()
    strip = lax.axis_index("strip")

    @pl.when(jnp.where(side == 0, strip > 0, strip < lax.axis_size("strip") - 1))
    def _():
        add = dot(next_ref[...].reshape(-1, wide), pair_taps(w_ref, 2 * side))
        for c in range(2):
            part_ref[c, :, side * (rows - 1)] += add[:, c * width : (c + 1) * width].reshape(slots, PAD, width)

    normalize(part_ref, tgain_ref, wq_ref, normed, tq, pl.ds(side * (rows - 1), 1))
    both = dot(normed[...].reshape(total, width), jnp.concatenate([wk_ref[...], wv_ref[...]], axis=1))
    tk[...] = both[:, :width].astype(BF16)
    tv[...] = both[:, width:].astype(BF16)
    group = rows * PAD
    pair = 2 * HEAD_DIM
    row = lax.broadcasted_iota(jnp.int32, (group, 2 * group), 0)
    col = lax.rem(lax.broadcasted_iota(jnp.int32, (group, 2 * group), 1), group)
    mask = jnp.where((row // PAD == col // PAD) & (lax.rem(col, PAD) < frames), 0.0, NEG).astype(F32)
    first = lax.broadcasted_iota(jnp.int32, (group, 2 * group), 1) < group
    ones = apart(jnp.ones((group, pair), BF16))
    tiles = [
        (g, slice(g * group, (g + 1) * group), slice(j * pair, (j + 1) * pair))
        for g in range(total // group)
        for j in range(width // pair)
    ]
    for g, rs, ls in tiles:
        query = tq[g // slots, g % slots, :, :, ls].reshape(group, pair)
        scores[rs, ls] = dot_t(query, apart(tk[rs, ls]))
    for _, rs, ls in tiles:
        s = scores[rs, ls] + mask
        top = jnp.where(
            first,
            jnp.max(jnp.where(first, s, NEG), axis=-1, keepdims=True),
            jnp.max(jnp.where(first, NEG, s), axis=-1, keepdims=True),
        )
        chances[rs, ls] = jnp.exp2((s - top) * (0.125 * LOG2E)).astype(BF16)
    for _, rs, ls in tiles:
        out = dot(chances[rs, ls], jnp.concatenate([apart(tv[rs, ls]), ones], axis=1))
        mixed[rs, ls] = (out[:, :pair] / out[:, pair:]).astype(BF16)
    after_ref[...] = part_ref[...] + dot(mixed[...], wo_ref[...]).reshape(after_ref.shape)
    nc = rms(after_ref[:, :half], xgain_ref[...]).astype(BF16).reshape(-1, width)
    query_ref[...] = dot(nc, xq_ref[...]).astype(BF16).reshape(query_ref.shape)


def cross_kernel(
    frames, slot_ref, gate_ref, after_ref, query_ref, own_ref, fetched_ref, swapped_ref, xo_ref, out_ref, keys, values, scores, chances, mixed, made, sems
):
    cols, slots, rows, _, width = after_ref.shape
    half = slots // 2
    even = first_row() == 1
    tokens = own_ref.shape[2]
    room = -(-tokens // 128) * 128
    group = cols * rows * PAD
    pair = 2 * HEAD_DIM
    first_page = lax.axis_index("req") * REQ_DEV
    for r in range(half):
        page = slot_ref[first_page + r]
        i = lax.rem(page, REQ_DEV)
        mine = page - i == first_page
        k = jnp.where(mine, own_ref[0, i], jnp.where(even, fetched_ref[i], swapped_ref[i]))
        v = jnp.where(mine, own_ref[1, i], jnp.where(even, swapped_ref[i], fetched_ref[i]))
        tail = jnp.zeros((room - tokens, width), BF16)
        keys[r] = jnp.concatenate([k, tail], axis=0)
        values[r] = jnp.concatenate([v, tail], axis=0)
    tiles = [(r, slice(j * pair, (j + 1) * pair), slice(2 * j * room, 2 * (j + 1) * room)) for r in range(half) for j in range(width // pair)]
    live = lax.rem(lax.broadcasted_iota(jnp.int32, (group, 2 * room), 1), room) < tokens
    ones = apart(jnp.ones((room, pair), BF16))
    for r, ls, ks in tiles:
        scores[r, :, ks] = dot_t(query_ref[:, r, :, :, ls].reshape(group, pair), apart(keys[r, :, ls]))
    for r, ls, ks in tiles:
        s = jnp.where(live, scores[r, :, ks], NEG)
        p = [jnp.exp2((t - jnp.max(t, axis=-1, keepdims=True)) * (0.125 * LOG2E)) for t in (s[:, :room], s[:, room:])]
        chances[r, :, ks] = jnp.concatenate(p, axis=1).astype(BF16)
    for r, ls, ks in tiles:
        out = dot(chances[r, :, ks], jnp.concatenate([apart(values[r, :, ls]), ones], axis=1))
        mixed[:, r, :, :, ls] = (out[:, :pair] / out[:, pair:]).astype(BF16).reshape(cols, rows, PAD, pair)
    frame = lax.broadcasted_iota(jnp.int32, (PAD, width), 0).astype(F32)
    scale = 1.0 + 2.0 * frame / (frames - 1)
    add = dot(mixed[...].reshape(-1, width), xo_ref[...]).reshape(cols, half, rows, PAD, width)
    copies = []
    for r in range(half):
        for c in range(cols):
            cond = (after_ref[c, r] + add[c, r]).astype(BF16).astype(F32)
            uncond = after_ref[c, half + r].astype(BF16).astype(F32)
            guided = jnp.where(gate_ref[r] == 1, uncond + scale * (cond - uncond), cond)
            for w in range(rows):
                made[r, w, :, c, :] = guided[w, :frames].astype(BF16)
        copies.append(pltpu.make_async_copy(made.at[r], out_ref.at[r], sems.at[r]))
        copies[r].start()
    for copy in copies:
        copy.wait()


def on_device(
    hidden_states, gate, context_slot, context_pages, conv_weight, conv_bias, conv_gain, temporal_gain,
    temporal_query, temporal_key, temporal_value, temporal_out, cross_gain, cross_query, cross_out,
):
    _, _, rows, cols, frames, width = hidden_states.shape
    slots = 2 * REQ_DEV
    count = lax.axis_size("req")
    partner_pairs = [(i, i ^ (count // 2)) for i in range(count)]
    strips = lax.axis_size("strip")
    near_pairs, next_pairs = (
        [p for i in range(start, strips - 1, 2) for p in ((i, i + 1), (i + 1, i))] for start in (0, 1)
    )

    vm = pl.BlockSpec(memory_space=pltpu.VMEM)
    sm = pl.BlockSpec(memory_space=pltpu.SMEM)
    any_ = pl.BlockSpec(memory_space=pl.ANY)
    total = cols * slots * rows * PAD
    wide = cols * width
    room = -(-context_pages.shape[2] // 128) * 128
    raw = hidden_states.reshape((slots, rows, cols, frames, width)).transpose(0, 1, 3, 2, 4)
    stored = context_pages.transpose(0, 2, 1, 3)
    half = pl.pallas_call(
        pages_kernel,
        out_shape=jax.ShapeDtypeStruct(stored.shape[1:], BF16),
        in_specs=[any_],
        out_specs=vm,
        scratch_shapes=[pltpu.SemaphoreType.DMA],
        compiler_params=pltpu.CompilerParams(vmem_limit_bytes=8 << 20),
        cost_estimate=cost(COSTP),
        name="pages",
    )(stored)
    fetched = lax.ppermute(half, "req", partner_pairs)
    swapped = lax.ppermute(fetched, "strip", near_pairs)
    fetched = fetched.transpose(1, 0, 2)
    swapped = swapped.transpose(1, 0, 2)
    row = jax.ShapeDtypeStruct((slots, PAD, wide), BF16)
    whole = jax.ShapeDtypeStruct((slots, rows, PAD, wide), BF16)
    edge_x, edge_act = pl.pallas_call(
        edge_kernel,
        out_shape=(row, row),
        in_specs=[vm] * 2,
        out_specs=(vm, vm),
        compiler_params=pltpu.CompilerParams(vmem_limit_bytes=8 << 20),
        cost_estimate=cost(COST0),
        name="edge",
    )(raw, conv_gain)
    near = lax.ppermute(edge_act, "strip", near_pairs)
    x, act, edge = pl.pallas_call(
        act_kernel,
        out_shape=(whole, whole, row),
        in_specs=[vm] * 4,
        out_specs=(vm,) * 3,
        compiler_params=pltpu.CompilerParams(vmem_limit_bytes=8 << 20),
        cost_estimate=cost(COST1),
        name="activate",
    )(raw, conv_gain, edge_x, edge_act)
    other = lax.ppermute(edge, "strip", next_pairs)
    grid = (cols, slots, rows, PAD, width)
    part, normed, queries = pl.pallas_call(
        conv_kernel,
        out_shape=(jax.ShapeDtypeStruct(grid, F32), jax.ShapeDtypeStruct(grid, BF16), jax.ShapeDtypeStruct(grid, BF16)),
        in_specs=[vm] * 7,
        out_specs=(vm,) * 3,
        scratch_shapes=[pltpu.VMEM((slots, rows + 2, PAD, wide), BF16)],
        compiler_params=pltpu.CompilerParams(vmem_limit_bytes=16 << 20),
        cost_estimate=cost(COST1),
        name="conv_own",
    )(x, act, near, conv_weight, conv_bias, temporal_gain, temporal_query)
    after, _, _, query = pl.pallas_call(
        functools.partial(time_kernel, frames),
        out_shape=(
            jax.ShapeDtypeStruct(grid, F32),
            jax.ShapeDtypeStruct(grid, BF16),
            jax.ShapeDtypeStruct(grid, BF16),
            jax.ShapeDtypeStruct((cols, REQ_DEV, rows, PAD, width), BF16),
        ),
        in_specs=[vm] * 12,
        out_specs=(vm,) * 4,
        scratch_shapes=[pltpu.VMEM((total, width), BF16)] * 3
        + [pltpu.VMEM((total, width // HEAD_DIM * rows * PAD), kind) for kind in (F32, BF16)],
        input_output_aliases={0: 0, 1: 1, 2: 2},
        compiler_params=pltpu.CompilerParams(vmem_limit_bytes=16 << 20),
        cost_estimate=cost(COST2),
        name="time_mix",
    )(
        part, normed, queries, other, conv_weight, temporal_gain, temporal_query, temporal_key, temporal_value,
        temporal_out, cross_gain, cross_query,
    )
    out = pl.pallas_call(
        functools.partial(cross_kernel, frames),
        out_shape=jax.ShapeDtypeStruct((REQ_DEV, rows, frames, cols, width), BF16),
        in_specs=[sm, sm] + [vm] * 6,
        out_specs=any_,
        scratch_shapes=[pltpu.VMEM((REQ_DEV, room, width), BF16)] * 2
        + [
            pltpu.VMEM((REQ_DEV, cols * rows * PAD, width // HEAD_DIM * room), F32),
            pltpu.VMEM((REQ_DEV, cols * rows * PAD, width // HEAD_DIM * room), BF16),
            pltpu.VMEM((cols, REQ_DEV, rows, PAD, width), BF16),
            pltpu.VMEM((REQ_DEV, rows, frames, cols, width), BF16),
            pltpu.SemaphoreType.DMA((REQ_DEV,)),
        ],
        compiler_params=pltpu.CompilerParams(vmem_limit_bytes=16 << 20),
        cost_estimate=cost(COST3),
        name="cross_mix",
    )(context_slot, gate, after, query, context_pages, fetched, swapped, cross_out)
    return out.transpose(0, 1, 3, 2, 4)


def solution(mesh):
    return jax.shard_map(
        on_device,
        mesh=mesh,
        in_specs=(
            P(None, "req", "strip", None, None, None),
            P("req"),
            P(),
            P(None, "req", None, None),
        )
        + (P(),) * 11,
        out_specs=P("req", "strip", None, None, None),
        check_vma=False,
    )
```

```python
import functools
import jax
import jax.numpy as jnp
from jax import lax
from jax.experimental import pallas as pl
from jax.experimental.pallas import tpu as pltpu
from jax.sharding import PartitionSpec as P

HEAD_DIM = 64
REQ_DEV = 2
PAD = 16
EPSILON = 1e-06
LOG2E = 1.4426950408889634
F32 = jnp.float32
BF16 = jnp.bfloat16
NEG = -1e30
COSTP, COST0, COST1, COST2, COST3 = 3 * 10**9, 16 * 10**9, 3 * 10**8, 6 * 10**9, 10**9


def cost(flops):
    return pl.CostEstimate(flops=flops, bytes_accessed=0, transcendentals=0)


def rms(x, gain):
    return x * lax.rsqrt(jnp.mean(x * x, axis=-1, keepdims=True) + EPSILON) * gain.reshape((1,) * (x.ndim - 1) + (-1,))


def silu(y):
    return y * (0.5 * jnp.tanh(0.5 * y) + 0.5)


def dot(a, b):
    return jnp.dot(a, b, preferred_element_type=F32)


def dot_t(a, b):
    return lax.dot_general(a, b, (((1,), (1,)), ((), ())), preferred_element_type=F32)


def pages_kernel(pages_ref, half_ref, sem):
    copy = pltpu.make_async_copy(pages_ref.at[1 - first_row()], half_ref, sem)
    copy.start()
    copy.wait()


def first_row():
    return 1 - lax.rem(lax.axis_index("strip"), 2)


def lay_out(raw_ref, gain_ref, s, r, x_ref, act_ref, *index):
    frames, cols, width = raw_ref.shape[2:]
    to = lax.broadcasted_iota(jnp.int32, (cols * PAD, cols * frames), 0)
    at = lax.broadcasted_iota(jnp.int32, (cols * PAD, cols * frames), 1)
    pick = (at == lax.rem(to, PAD) * cols + to // PAD) & (lax.rem(to, PAD) < frames)
    rows = dot(pick.astype(F32).astype(BF16), raw_ref[s, r].reshape(frames * cols, width))
    for c in range(cols):
        ls = slice(c * width, (c + 1) * width)
        one = rows[c * PAD : (c + 1) * PAD]
        x_ref[(*index, slice(None), ls)] = one.astype(BF16)
        act_ref[(*index, slice(None), ls)] = silu(rms(one, gain_ref[...])).astype(BF16)


def edge_kernel(raw_ref, gain_ref, x_ref, act_ref):
    slots, rows = raw_ref.shape[:2]
    r = first_row() * (rows - 1)
    for s in range(slots):
        lay_out(raw_ref, gain_ref, s, r, x_ref, act_ref, s)


def act_kernel(raw_ref, gain_ref, edge_x_ref, edge_act_ref, x_ref, act_ref, edge_ref):
    slots, rows = raw_ref.shape[:2]
    done = first_row() * (rows - 1)
    other = rows - 1 - done
    x_ref[:, done] = edge_x_ref[...]
    act_ref[:, done] = edge_act_ref[...]
    for s in range(slots):
        for r in (other, *range(1, rows - 1)):
            lay_out(raw_ref, gain_ref, s, r, x_ref, act_ref, s, r)
        edge_ref[s] = act_ref[s, other]


def conv_kernel(
    x_ref, act_ref, near_ref, w_ref, bias_ref, tgain_ref, wq_ref, out_ref, normed_ref, tq_ref, ext
):
    slots, rows, _, wide = x_ref.shape
    width = wide // 2
    side = 2 * first_row()
    ext[:, 1 : rows + 1] = act_ref[...]
    ext[:, side // 2 * (rows + 1)] = near_ref[...]
    both = jnp.concatenate(
        [ext[:, 1 : rows + 1].reshape(-1, wide), ext[:, pl.ds(side, rows)].reshape(-1, wide)], axis=-1
    )
    inner = ext[:, pl.ds(2 - side // 2, rows - 1)].reshape(-1, wide)
    inner_rows = pl.ds(side // 2, rows - 1)
    weights = jnp.concatenate([pair_taps(w_ref, 1), pair_taps(w_ref, side)], axis=0)
    mid = dot(both, weights)
    rest = dot(inner, pair_taps(w_ref, 2 - side))
    for c in range(2):
        ls = slice(c * width, (c + 1) * width)
        out_ref[c] = (
            x_ref[:, :, :, ls].astype(F32) + bias_ref[...].reshape(1, 1, 1, width) + mid[:, ls].reshape(slots, rows, PAD, width)
        )
        out_ref[c, :, inner_rows] += rest[:, ls].reshape(slots, rows - 1, PAD, width)
    normalize(out_ref, tgain_ref, wq_ref, normed_ref, tq_ref, pl.ds(side // 2, rows - 1))


def normalize(field_ref, gain_ref, wq_ref, normed_ref, tq_ref, place):
    field = rms(field_ref[:, :, place], gain_ref[...]).astype(BF16)
    normed_ref[:, :, place] = field
    tq_ref[:, :, place] = dot(field.reshape(-1, field.shape[-1]), wq_ref[...]).astype(BF16).reshape(field.shape)


def pair_taps(w_ref, dr):
    wide = 2 * w_ref.shape[2]
    return jnp.concatenate([w_ref[dr, 1 - c : 3 - c].reshape(wide, wide // 2) for c in range(2)], axis=1)


def apart(x):
    first = lax.broadcasted_iota(jnp.int32, x.shape, 1) < HEAD_DIM
    zero = jnp.zeros_like(x)
    return jnp.concatenate([jnp.where(first, x, zero), jnp.where(first, zero, x)], axis=0)


def time_kernel(
    frames, slot_ref, gate_ref, part_ref, normed, tq, next_ref, w_ref, tgain_ref, wq_ref, wk_ref, wv_ref, wo_ref,
    xgain_ref, xq_ref, after_ref, _normed, _tq, query_ref, choice_ref, live_ref, tk, tv, mixed, scores, chances,
    slot, gate, sems
):
    loads = [
        pltpu.make_async_copy(slot_ref, slot, sems.at[0]),
        pltpu.make_async_copy(gate_ref, gate, sems.at[1]),
    ]
    for load in loads:
        load.start()
    cols, slots, rows, _, width = part_ref.shape
    wide = 2 * width
    half = slots // 2
    total = cols * slots * rows * PAD
    side = 1 - first_row()
    strip = lax.axis_index("strip")

    @pl.when(jnp.where(side == 0, strip > 0, strip < lax.axis_size("strip") - 1))
    def _():
        add = dot(next_ref[...].reshape(-1, wide), pair_taps(w_ref, 2 * side))
        for c in range(2):
            part_ref[c, :, side * (rows - 1)] += add[:, c * width : (c + 1) * width].reshape(slots, PAD, width)

    normalize(part_ref, tgain_ref, wq_ref, normed, tq, pl.ds(side * (rows - 1), 1))
    both = dot(normed[...].reshape(total, width), jnp.concatenate([wk_ref[...], wv_ref[...]], axis=1))
    tk[...] = both[:, :width].astype(BF16)
    tv[...] = both[:, width:].astype(BF16)
    group = rows * PAD
    pair = 2 * HEAD_DIM
    row = lax.broadcasted_iota(jnp.int32, (group, 2 * group), 0)
    col = lax.rem(lax.broadcasted_iota(jnp.int32, (group, 2 * group), 1), group)
    mask = jnp.where((row // PAD == col // PAD) & (lax.rem(col, PAD) < frames), 0.0, NEG).astype(F32)
    first = lax.broadcasted_iota(jnp.int32, (group, 2 * group), 1) < group
    ones = apart(jnp.ones((group, pair), BF16))
    tiles = [
        (g, slice(g * group, (g + 1) * group), slice(j * pair, (j + 1) * pair))
        for g in range(total // group)
        for j in range(width // pair)
    ]
    for g, rs, ls in tiles:
        query = tq[g // slots, g % slots, :, :, ls].reshape(group, pair)
        scores[rs, ls] = dot_t(query, apart(tk[rs, ls]))
    for _, rs, ls in tiles:
        s = scores[rs, ls] + mask
        top = jnp.where(
            first,
            jnp.max(jnp.where(first, s, NEG), axis=-1, keepdims=True),
            jnp.max(jnp.where(first, NEG, s), axis=-1, keepdims=True),
        )
        chances[rs, ls] = jnp.exp2((s - top) * (0.125 * LOG2E)).astype(BF16)
    for _, rs, ls in tiles:
        out = dot(chances[rs, ls], jnp.concatenate([apart(tv[rs, ls]), ones], axis=1))
        mixed[rs, ls] = (out[:, :pair] / out[:, pair:]).astype(BF16)
    after_ref[...] = part_ref[...] + dot(mixed[...], wo_ref[...]).reshape(after_ref.shape)
    nc = rms(after_ref[:, :half], xgain_ref[...]).astype(BF16).reshape(-1, width)
    query_ref[...] = dot(nc, xq_ref[...]).astype(BF16).reshape(query_ref.shape)
    for load in loads:
        load.wait()
    first_page = lax.axis_index("req") * REQ_DEV
    for r in range(half):
        page = slot[first_page + r]
        i = lax.rem(page, REQ_DEV)
        place = i + jnp.where(page - i == first_page, 0, REQ_DEV)
        for j in range(2 * REQ_DEV):
            choice_ref[r, j] = jnp.full(choice_ref.shape[2:], jnp.where(place == j, 1.0, 0.0), F32).astype(BF16)
        live_ref[r] = jnp.full(live_ref.shape[1:], jnp.where(gate[r] == 1, 1.0, 0.0), F32)


def cross_kernel(
    frames, choice_ref, live_ref, after_ref, query_ref, own_ref, fetched_ref, swapped_ref, xo_ref, out_ref, keys, values, scores, chances, mixed, made, sems
):
    cols, slots, rows, _, width = after_ref.shape
    half = slots // 2
    even = first_row() == 1
    tokens = own_ref.shape[2]
    room = -(-tokens // 128) * 128
    group = cols * rows * PAD
    pair = 2 * HEAD_DIM
    for r in range(half):
        k = v = jnp.zeros((tokens, width), BF16)
        for i in range(REQ_DEV):
            mine, theirs = (choice_ref[r, j, 0:1] for j in (i, REQ_DEV + i))
            far_k = jnp.where(even, fetched_ref[i], swapped_ref[i])
            far_v = jnp.where(even, swapped_ref[i], fetched_ref[i])
            k += own_ref[0, i] * mine + far_k * theirs
            v += own_ref[1, i] * mine + far_v * theirs
        tail = jnp.zeros((room - tokens, width), BF16)
        keys[r] = jnp.concatenate([k, tail], axis=0)
        values[r] = jnp.concatenate([v, tail], axis=0)
    tiles = [(r, slice(j * pair, (j + 1) * pair), slice(2 * j * room, 2 * (j + 1) * room)) for r in range(half) for j in range(width // pair)]
    live = lax.rem(lax.broadcasted_iota(jnp.int32, (group, 2 * room), 1), room) < tokens
    ones = apart(jnp.ones((room, pair), BF16))
    for r, ls, ks in tiles:
        scores[r, :, ks] = dot_t(query_ref[:, r, :, :, ls].reshape(group, pair), apart(keys[r, :, ls]))
    for r, ls, ks in tiles:
        s = jnp.where(live, scores[r, :, ks], NEG)
        p = [jnp.exp2((t - jnp.max(t, axis=-1, keepdims=True)) * (0.125 * LOG2E)) for t in (s[:, :room], s[:, room:])]
        chances[r, :, ks] = jnp.concatenate(p, axis=1).astype(BF16)
    for r, ls, ks in tiles:
        out = dot(chances[r, :, ks], jnp.concatenate([apart(values[r, :, ls]), ones], axis=1))
        mixed[:, r, :, :, ls] = (out[:, :pair] / out[:, pair:]).astype(BF16).reshape(cols, rows, PAD, pair)
    frame = lax.broadcasted_iota(jnp.int32, (PAD, width), 0).astype(F32)
    scale = 1.0 + 2.0 * frame / (frames - 1)
    add = dot(mixed[...].reshape(-1, width), xo_ref[...]).reshape(cols, half, rows, PAD, width)
    copies = []
    for r in range(half):
        for c in range(cols):
            cond = (after_ref[c, r] + add[c, r]).astype(BF16).astype(F32)
            uncond = after_ref[c, half + r].astype(BF16).astype(F32)
            guided = jnp.where(live_ref[r] == 1.0, uncond + scale * (cond - uncond), cond)
            for w in range(rows):
                made[r, w, :, c, :] = guided[w, :frames].astype(BF16)
        copies.append(pltpu.make_async_copy(made.at[r], out_ref.at[r], sems.at[r]))
        copies[r].start()
    for copy in copies:
        copy.wait()


def on_device(
    hidden_states, gate, context_slot, context_pages, conv_weight, conv_bias, conv_gain, temporal_gain,
    temporal_query, temporal_key, temporal_value, temporal_out, cross_gain, cross_query, cross_out,
):
    _, _, rows, cols, frames, width = hidden_states.shape
    slots = 2 * REQ_DEV
    count = lax.axis_size("req")
    partner_pairs = [(i, i ^ (count // 2)) for i in range(count)]
    strips = lax.axis_size("strip")
    near_pairs, next_pairs = (
        [p for i in range(start, strips - 1, 2) for p in ((i, i + 1), (i + 1, i))] for start in (0, 1)
    )

    vm = pl.BlockSpec(memory_space=pltpu.VMEM)
    any_ = pl.BlockSpec(memory_space=pl.ANY)
    total = cols * slots * rows * PAD
    wide = cols * width
    room = -(-context_pages.shape[2] // 128) * 128
    raw = hidden_states.reshape((slots, rows, cols, frames, width)).transpose(0, 1, 3, 2, 4)
    stored = context_pages.transpose(0, 2, 1, 3)
    half = pl.pallas_call(
        pages_kernel,
        out_shape=jax.ShapeDtypeStruct(stored.shape[1:], BF16),
        in_specs=[any_],
        out_specs=vm,
        scratch_shapes=[pltpu.SemaphoreType.DMA],
        compiler_params=pltpu.CompilerParams(vmem_limit_bytes=8 << 20),
        cost_estimate=cost(COSTP),
        name="pages",
    )(stored)
    fetched = lax.ppermute(half, "req", partner_pairs)
    swapped = lax.ppermute(fetched, "strip", near_pairs)
    fetched = fetched.transpose(1, 0, 2)
    swapped = swapped.transpose(1, 0, 2)
    row = jax.ShapeDtypeStruct((slots, PAD, wide), BF16)
    whole = jax.ShapeDtypeStruct((slots, rows, PAD, wide), BF16)
    edge_x, edge_act = pl.pallas_call(
        edge_kernel,
        out_shape=(row, row),
        in_specs=[vm] * 2,
        out_specs=(vm, vm),
        compiler_params=pltpu.CompilerParams(vmem_limit_bytes=8 << 20),
        cost_estimate=cost(COST0),
        name="edge",
    )(raw, conv_gain)
    near = lax.ppermute(edge_act, "strip", near_pairs)
    x, act, edge = pl.pallas_call(
        act_kernel,
        out_shape=(whole, whole, row),
        in_specs=[vm] * 4,
        out_specs=(vm,) * 3,
        compiler_params=pltpu.CompilerParams(vmem_limit_bytes=8 << 20),
        cost_estimate=cost(COST1),
        name="activate",
    )(raw, conv_gain, edge_x, edge_act)
    other = lax.ppermute(edge, "strip", next_pairs)
    grid = (cols, slots, rows, PAD, width)
    part, normed, queries = pl.pallas_call(
        conv_kernel,
        out_shape=(jax.ShapeDtypeStruct(grid, F32), jax.ShapeDtypeStruct(grid, BF16), jax.ShapeDtypeStruct(grid, BF16)),
        in_specs=[vm] * 7,
        out_specs=(vm,) * 3,
        scratch_shapes=[pltpu.VMEM((slots, rows + 2, PAD, wide), BF16)],
        compiler_params=pltpu.CompilerParams(vmem_limit_bytes=16 << 20),
        cost_estimate=cost(COST1),
        name="conv_own",
    )(x, act, near, conv_weight, conv_bias, temporal_gain, temporal_query)
    after, _, _, query, choice, live = pl.pallas_call(
        functools.partial(time_kernel, frames),
        out_shape=(
            jax.ShapeDtypeStruct(grid, F32),
            jax.ShapeDtypeStruct(grid, BF16),
            jax.ShapeDtypeStruct(grid, BF16),
            jax.ShapeDtypeStruct((cols, REQ_DEV, rows, PAD, width), BF16),
            jax.ShapeDtypeStruct((REQ_DEV, 2 * REQ_DEV, PAD, width), BF16),
            jax.ShapeDtypeStruct((REQ_DEV, PAD, width), F32),
        ),
        in_specs=[any_] * 2 + [vm] * 12,
        out_specs=(vm,) * 6,
        scratch_shapes=[pltpu.VMEM((total, width), BF16)] * 3
        + [pltpu.VMEM((total, width // HEAD_DIM * rows * PAD), kind) for kind in (F32, BF16)]
        + [pltpu.SMEM(context_slot.shape, jnp.int32), pltpu.SMEM(gate.shape, jnp.int32), pltpu.SemaphoreType.DMA((2,))],
        input_output_aliases={2: 0, 3: 1, 4: 2},
        compiler_params=pltpu.CompilerParams(vmem_limit_bytes=16 << 20),
        cost_estimate=cost(COST2),
        name="time_mix",
    )(
        context_slot, gate, part, normed, queries, other, conv_weight, temporal_gain, temporal_query, temporal_key, temporal_value,
        temporal_out, cross_gain, cross_query,
    )
    out = pl.pallas_call(
        functools.partial(cross_kernel, frames),
        out_shape=jax.ShapeDtypeStruct((REQ_DEV, rows, frames, cols, width), BF16),
        in_specs=[vm] * 8,
        out_specs=any_,
        scratch_shapes=[pltpu.VMEM((REQ_DEV, room, width), BF16)] * 2
        + [
            pltpu.VMEM((REQ_DEV, cols * rows * PAD, width // HEAD_DIM * room), F32),
            pltpu.VMEM((REQ_DEV, cols * rows * PAD, width // HEAD_DIM * room), BF16),
            pltpu.VMEM((cols, REQ_DEV, rows, PAD, width), BF16),
            pltpu.VMEM((REQ_DEV, rows, frames, cols, width), BF16),
            pltpu.SemaphoreType.DMA((REQ_DEV,)),
        ],
        compiler_params=pltpu.CompilerParams(vmem_limit_bytes=16 << 20),
        cost_estimate=cost(COST3),
        name="cross_mix",
    )(choice, live, after, query, context_pages, fetched, swapped, cross_out)
    return out.transpose(0, 1, 3, 2, 4)


def solution(mesh):
    return jax.shard_map(
        on_device,
        mesh=mesh,
        in_specs=(
            P(None, "req", "strip", None, None, None),
            P("req"),
            P(),
            P(None, "req", None, None),
        )
        + (P(),) * 11,
        out_specs=P("req", "strip", None, None, None),
        check_vma=False,
    )
```

```python
import functools
import jax
import jax.numpy as jnp
from jax import lax
from jax.experimental import pallas as pl
from jax.experimental.layout import Layout, with_layout_constraint
from jax.experimental.pallas import tpu as pltpu
from jax.sharding import PartitionSpec as P

HEAD_DIM = 64
REQ_DEV = 2
PAD = 16
EPSILON = 1e-06
LOG2E = 1.4426950408889634
F32 = jnp.float32
BF16 = jnp.bfloat16
NEG = -1e30
COSTP, COST0, COST1, COST2, COST3 = 3 * 10**9, 16 * 10**9, 3 * 10**8, 6 * 10**9, 10**9


def cost(flops):
    return pl.CostEstimate(flops=flops, bytes_accessed=0, transcendentals=0)


def rms(x, gain):
    return x * lax.rsqrt(jnp.mean(x * x, axis=-1, keepdims=True) + EPSILON) * gain.reshape((1,) * (x.ndim - 1) + (-1,))


def silu(y):
    return y * (0.5 * jnp.tanh(0.5 * y) + 0.5)


def dot(a, b):
    return jnp.dot(a, b, preferred_element_type=F32)


def dot_t(a, b):
    return lax.dot_general(a, b, (((1,), (1,)), ((), ())), preferred_element_type=F32)


def pages_kernel(pages_ref, half_ref, sem):
    copy = pltpu.make_async_copy(pages_ref.at[1 - first_row()], half_ref, sem)
    copy.start()
    copy.wait()


def first_row():
    return 1 - lax.rem(lax.axis_index("strip"), 2)


def lay_out(raw_ref, gain_ref, s, r, x_ref, act_ref, *index):
    frames, cols, width = raw_ref.shape[2:]
    to = lax.broadcasted_iota(jnp.int32, (cols * PAD, cols * frames), 0)
    at = lax.broadcasted_iota(jnp.int32, (cols * PAD, cols * frames), 1)
    pick = (at == lax.rem(to, PAD) * cols + to // PAD) & (lax.rem(to, PAD) < frames)
    rows = dot(pick.astype(F32).astype(BF16), raw_ref[s, r].reshape(frames * cols, width))
    for c in range(cols):
        ls = slice(c * width, (c + 1) * width)
        one = rows[c * PAD : (c + 1) * PAD]
        x_ref[(*index, slice(None), ls)] = one.astype(BF16)
        act_ref[(*index, slice(None), ls)] = silu(rms(one, gain_ref[...])).astype(BF16)


def edge_kernel(raw_ref, gain_ref, x_ref, act_ref):
    slots, rows = raw_ref.shape[:2]
    r = first_row() * (rows - 1)
    for s in range(slots):
        lay_out(raw_ref, gain_ref, s, r, x_ref, act_ref, s)


def act_kernel(raw_ref, gain_ref, edge_x_ref, edge_act_ref, x_ref, act_ref, edge_ref):
    slots, rows = raw_ref.shape[:2]
    done = first_row() * (rows - 1)
    other = rows - 1 - done
    x_ref[:, done] = edge_x_ref[...]
    act_ref[:, done] = edge_act_ref[...]
    for s in range(slots):
        for r in (other, *range(1, rows - 1)):
            lay_out(raw_ref, gain_ref, s, r, x_ref, act_ref, s, r)
        edge_ref[s] = act_ref[s, other]


def conv_kernel(x_ref, act_ref, near_ref, w_ref, bias_ref, out_ref, ext):
    slots, rows, _, wide = x_ref.shape
    width = wide // 2
    side = 2 * first_row()
    ext[:, 1 : rows + 1] = act_ref[...]
    ext[:, side // 2 * (rows + 1)] = near_ref[...]
    both = jnp.concatenate(
        [ext[:, 1 : rows + 1].reshape(-1, wide), ext[:, pl.ds(side, rows)].reshape(-1, wide)], axis=-1
    )
    inner = ext[:, pl.ds(2 - side // 2, rows - 1)].reshape(-1, wide)
    inner_rows = pl.ds(side // 2, rows - 1)
    weights = jnp.concatenate([pair_taps(w_ref, 1), pair_taps(w_ref, side)], axis=0)
    mid = dot(both, weights)
    rest = dot(inner, pair_taps(w_ref, 2 - side))
    for c in range(2):
        ls = slice(c * width, (c + 1) * width)
        out_ref[c] = (
            x_ref[:, :, :, ls].astype(F32) + bias_ref[...].reshape(1, 1, 1, width) + mid[:, ls].reshape(slots, rows, PAD, width)
        )
        out_ref[c, :, inner_rows] += rest[:, ls].reshape(slots, rows - 1, PAD, width)


def pair_taps(w_ref, dr):
    wide = 2 * w_ref.shape[2]
    return jnp.concatenate([w_ref[dr, 1 - c : 3 - c].reshape(wide, wide // 2) for c in range(2)], axis=1)


def apart(x):
    first = lax.broadcasted_iota(jnp.int32, x.shape, 1) < HEAD_DIM
    zero = jnp.zeros_like(x)
    return jnp.concatenate([jnp.where(first, x, zero), jnp.where(first, zero, x)], axis=0)


def time_kernel(
    frames, slot_ref, gate_ref, part_ref, next_ref, w_ref, tgain_ref, wq_ref, wk_ref, wv_ref, wo_ref,
    xgain_ref, xq_ref, after_ref, query_ref, choice_ref, live_ref, normed, tq, tk, tv, mixed, scores, chances,
    slot, gate, sems
):
    loads = [
        pltpu.make_async_copy(slot_ref, slot, sems.at[0]),
        pltpu.make_async_copy(gate_ref, gate, sems.at[1]),
    ]
    for load in loads:
        load.start()
    cols, slots, rows, _, width = part_ref.shape
    wide = 2 * width
    half = slots // 2
    total = cols * slots * rows * PAD
    side = 1 - first_row()
    strip = lax.axis_index("strip")

    @pl.when(jnp.where(side == 0, strip > 0, strip < lax.axis_size("strip") - 1))
    def _():
        add = dot(next_ref[...].reshape(-1, wide), pair_taps(w_ref, 2 * side))
        for c in range(2):
            part_ref[c, :, side * (rows - 1)] += add[:, c * width : (c + 1) * width].reshape(slots, PAD, width)

    normed[...] = rms(part_ref[...].reshape(total, width), tgain_ref[...]).astype(BF16)
    every = dot(normed[...], jnp.concatenate([wq_ref[...], wk_ref[...], wv_ref[...]], axis=1))
    for i, field in enumerate((tq, tk, tv)):
        field[...] = every[:, i * width : (i + 1) * width].astype(BF16)
    group = rows * PAD
    pair = 2 * HEAD_DIM
    row = lax.broadcasted_iota(jnp.int32, (group, 2 * group), 0)
    col = lax.rem(lax.broadcasted_iota(jnp.int32, (group, 2 * group), 1), group)
    mask = jnp.where((row // PAD == col // PAD) & (lax.rem(col, PAD) < frames), 0.0, NEG).astype(F32)
    first = lax.broadcasted_iota(jnp.int32, (group, 2 * group), 1) < group
    ones = apart(jnp.ones((group, pair), BF16))
    tiles = [
        (g, slice(g * group, (g + 1) * group), slice(j * pair, (j + 1) * pair))
        for g in range(total // group)
        for j in range(width // pair)
    ]
    for g, rs, ls in tiles:
        scores[rs, ls] = dot_t(tq[rs, ls], apart(tk[rs, ls]))
    for _, rs, ls in tiles:
        s = scores[rs, ls] + mask
        top = jnp.where(
            first,
            jnp.max(jnp.where(first, s, NEG), axis=-1, keepdims=True),
            jnp.max(jnp.where(first, NEG, s), axis=-1, keepdims=True),
        )
        chances[rs, ls] = jnp.exp2((s - top) * (0.125 * LOG2E)).astype(BF16)
    for _, rs, ls in tiles:
        out = dot(chances[rs, ls], jnp.concatenate([apart(tv[rs, ls]), ones], axis=1))
        mixed[rs, ls] = (out[:, :pair] / out[:, pair:]).astype(BF16)
    after_ref[...] = part_ref[...] + dot(mixed[...], wo_ref[...]).reshape(after_ref.shape)
    nc = rms(after_ref[:, :half], xgain_ref[...]).astype(BF16).reshape(-1, width)
    query_ref[...] = dot(nc, xq_ref[...]).astype(BF16).reshape(query_ref.shape)
    for load in loads:
        load.wait()
    first_page = lax.axis_index("req") * REQ_DEV
    for r in range(half):
        page = slot[first_page + r]
        i = lax.rem(page, REQ_DEV)
        place = i + jnp.where(page - i == first_page, 0, REQ_DEV)
        for j in range(2 * REQ_DEV):
            choice_ref[r, j] = jnp.full(choice_ref.shape[2:], jnp.where(place == j, 1.0, 0.0), F32).astype(BF16)
        live_ref[r] = jnp.full(live_ref.shape[1:], jnp.where(gate[r] == 1, 1.0, 0.0), F32)


def cross_kernel(
    frames, choice_ref, live_ref, after_ref, query_ref, own_ref, fetched_ref, swapped_ref, xo_ref, out_ref, keys, values, scores, chances, mixed, made, sems
):
    cols, slots, rows, _, width = after_ref.shape
    half = slots // 2
    even = first_row() == 1
    tokens = own_ref.shape[2]
    room = -(-tokens // 128) * 128
    group = cols * rows * PAD
    pair = 2 * HEAD_DIM
    for r in range(half):
        k = v = jnp.zeros((tokens, width), BF16)
        for i in range(REQ_DEV):
            mine, theirs = (choice_ref[r, j, 0:1] for j in (i, REQ_DEV + i))
            far_k = jnp.where(even, fetched_ref[i], swapped_ref[i])
            far_v = jnp.where(even, swapped_ref[i], fetched_ref[i])
            k += own_ref[0, i] * mine + far_k * theirs
            v += own_ref[1, i] * mine + far_v * theirs
        tail = jnp.zeros((room - tokens, width), BF16)
        keys[r] = jnp.concatenate([k, tail], axis=0)
        values[r] = jnp.concatenate([v, tail], axis=0)
    tiles = [(r, slice(j * pair, (j + 1) * pair), slice(2 * j * room, 2 * (j + 1) * room)) for r in range(half) for j in range(width // pair)]
    live = lax.rem(lax.broadcasted_iota(jnp.int32, (group, 2 * room), 1), room) < tokens
    ones = apart(jnp.ones((room, pair), BF16))
    for r, ls, ks in tiles:
        scores[r, :, ks] = dot_t(query_ref[:, r, :, :, ls].reshape(group, pair), apart(keys[r, :, ls]))
    for r, ls, ks in tiles:
        s = jnp.where(live, scores[r, :, ks], NEG)
        p = [jnp.exp2((t - jnp.max(t, axis=-1, keepdims=True)) * (0.125 * LOG2E)) for t in (s[:, :room], s[:, room:])]
        chances[r, :, ks] = jnp.concatenate(p, axis=1).astype(BF16)
    for r, ls, ks in tiles:
        out = dot(chances[r, :, ks], jnp.concatenate([apart(values[r, :, ls]), ones], axis=1))
        mixed[:, r, :, :, ls] = (out[:, :pair] / out[:, pair:]).astype(BF16).reshape(cols, rows, PAD, pair)
    frame = lax.broadcasted_iota(jnp.int32, (PAD, width), 0).astype(F32)
    scale = 1.0 + 2.0 * frame / (frames - 1)
    add = dot(mixed[...].reshape(-1, width), xo_ref[...]).reshape(cols, half, rows, PAD, width)
    copies = []
    for r in range(half):
        for c in range(cols):
            cond = (after_ref[c, r] + add[c, r]).astype(BF16).astype(F32)
            uncond = after_ref[c, half + r].astype(BF16).astype(F32)
            guided = jnp.where(live_ref[r] == 1.0, uncond + scale * (cond - uncond), cond)
            for w in range(rows):
                made[r, w, :, c, :] = guided[w, :frames].astype(BF16)
        copies.append(pltpu.make_async_copy(made.at[r], out_ref.at[r], sems.at[r]))
        copies[r].start()
    for copy in copies:
        copy.wait()


def on_device(
    hidden_states, gate, context_slot, context_pages, conv_weight, conv_bias, conv_gain, temporal_gain,
    temporal_query, temporal_key, temporal_value, temporal_out, cross_gain, cross_query, cross_out,
):
    _, _, rows, cols, frames, width = hidden_states.shape
    slots = 2 * REQ_DEV
    count = lax.axis_size("req")
    partner_pairs = [(i, i ^ (count // 2)) for i in range(count)]
    strips = lax.axis_size("strip")
    near_pairs, next_pairs = (
        [p for i in range(start, strips - 1, 2) for p in ((i, i + 1), (i + 1, i))] for start in (0, 1)
    )

    vm = pl.BlockSpec(memory_space=pltpu.VMEM)
    any_ = pl.BlockSpec(memory_space=pl.ANY)
    total = cols * slots * rows * PAD
    wide = cols * width
    room = -(-context_pages.shape[2] // 128) * 128
    raw = hidden_states.reshape((slots, rows, cols, frames, width)).transpose(0, 1, 3, 2, 4)
    stored = context_pages.transpose(0, 2, 1, 3)
    half = pl.pallas_call(
        pages_kernel,
        out_shape=jax.ShapeDtypeStruct(stored.shape[1:], BF16),
        in_specs=[any_],
        out_specs=vm,
        scratch_shapes=[pltpu.SemaphoreType.DMA],
        compiler_params=pltpu.CompilerParams(vmem_limit_bytes=8 << 20),
        cost_estimate=cost(COSTP),
        name="pages",
    )(stored)
    keep = Layout(major_to_minor=(0, 1, 2))
    fetched = with_layout_constraint(lax.ppermute(half, "req", partner_pairs), keep)
    swapped = with_layout_constraint(lax.ppermute(fetched, "strip", near_pairs), keep)
    fetched = fetched.transpose(1, 0, 2)
    swapped = swapped.transpose(1, 0, 2)
    row = jax.ShapeDtypeStruct((slots, PAD, wide), BF16)
    whole = jax.ShapeDtypeStruct((slots, rows, PAD, wide), BF16)
    edge_x, edge_act = pl.pallas_call(
        edge_kernel,
        out_shape=(row, row),
        in_specs=[vm] * 2,
        out_specs=(vm, vm),
        compiler_params=pltpu.CompilerParams(vmem_limit_bytes=8 << 20),
        cost_estimate=cost(COST0),
        name="edge",
    )(raw, conv_gain)
    near = lax.ppermute(edge_act, "strip", near_pairs)
    x, act, edge = pl.pallas_call(
        act_kernel,
        out_shape=(whole, whole, row),
        in_specs=[vm] * 4,
        out_specs=(vm,) * 3,
        compiler_params=pltpu.CompilerParams(vmem_limit_bytes=8 << 20),
        cost_estimate=cost(COST1),
        name="activate",
    )(raw, conv_gain, edge_x, edge_act)
    other = lax.ppermute(edge, "strip", next_pairs)
    grid = (cols, slots, rows, PAD, width)
    part = pl.pallas_call(
        conv_kernel,
        out_shape=jax.ShapeDtypeStruct(grid, F32),
        in_specs=[vm] * 5,
        out_specs=vm,
        scratch_shapes=[pltpu.VMEM((slots, rows + 2, PAD, wide), BF16)],
        compiler_params=pltpu.CompilerParams(vmem_limit_bytes=16 << 20),
        cost_estimate=cost(COST1),
        name="conv_own",
    )(x, act, near, conv_weight, conv_bias)
    after, query, choice, live = pl.pallas_call(
        functools.partial(time_kernel, frames),
        out_shape=(
            jax.ShapeDtypeStruct(grid, F32),
            jax.ShapeDtypeStruct((cols, REQ_DEV, rows, PAD, width), BF16),
            jax.ShapeDtypeStruct((REQ_DEV, 2 * REQ_DEV, PAD, width), BF16),
            jax.ShapeDtypeStruct((REQ_DEV, PAD, width), F32),
        ),
        in_specs=[any_] * 2 + [vm] * 10,
        out_specs=(vm,) * 4,
        scratch_shapes=[pltpu.VMEM((total, width), BF16)] * 5
        + [pltpu.VMEM((total, width // HEAD_DIM * rows * PAD), kind) for kind in (F32, BF16)]
        + [pltpu.SMEM(context_slot.shape, jnp.int32), pltpu.SMEM(gate.shape, jnp.int32), pltpu.SemaphoreType.DMA((2,))],
        input_output_aliases={2: 0},
        compiler_params=pltpu.CompilerParams(vmem_limit_bytes=16 << 20),
        cost_estimate=cost(COST2),
        name="time_mix",
    )(
        context_slot, gate, part, other, conv_weight, temporal_gain, temporal_query, temporal_key, temporal_value,
        temporal_out, cross_gain, cross_query,
    )
    out = pl.pallas_call(
        functools.partial(cross_kernel, frames),
        out_shape=jax.ShapeDtypeStruct((REQ_DEV, rows, frames, cols, width), BF16),
        in_specs=[vm] * 8,
        out_specs=any_,
        scratch_shapes=[pltpu.VMEM((REQ_DEV, room, width), BF16)] * 2
        + [
            pltpu.VMEM((REQ_DEV, cols * rows * PAD, width // HEAD_DIM * room), F32),
            pltpu.VMEM((REQ_DEV, cols * rows * PAD, width // HEAD_DIM * room), BF16),
            pltpu.VMEM((cols, REQ_DEV, rows, PAD, width), BF16),
            pltpu.VMEM((REQ_DEV, rows, frames, cols, width), BF16),
            pltpu.SemaphoreType.DMA((REQ_DEV,)),
        ],
        compiler_params=pltpu.CompilerParams(vmem_limit_bytes=16 << 20),
        cost_estimate=cost(COST3),
        name="cross_mix",
    )(choice, live, after, query, context_pages, fetched, swapped, cross_out)
    return out.transpose(0, 1, 3, 2, 4)


def solution(mesh):
    return jax.shard_map(
        on_device,
        mesh=mesh,
        in_specs=(
            P(None, "req", "strip", None, None, None),
            P("req"),
            P(),
            P(None, "req", None, None),
        )
        + (P(),) * 11,
        out_specs=P("req", "strip", None, None, None),
        check_vma=False,
    )
```

```python
import functools
import jax
import jax.numpy as jnp
from jax import lax
from jax.experimental import pallas as pl
from jax.experimental.layout import Layout, with_layout_constraint
from jax.experimental.pallas import tpu as pltpu
from jax.sharding import PartitionSpec as P

HEAD_DIM = 64
REQ_DEV = 2
PAD = 16
EPSILON = 1e-06
LOG2E = 1.4426950408889634
F32 = jnp.float32
BF16 = jnp.bfloat16
NEG = -1e30
COSTP, COST0, COST1, COST2, COST3 = 3 * 10**9, 16 * 10**9, 3 * 10**8, 6 * 10**9, 10**9


def cost(flops):
    return pl.CostEstimate(flops=flops, bytes_accessed=0, transcendentals=0)


def rms(x, gain):
    return x * lax.rsqrt(jnp.mean(x * x, axis=-1, keepdims=True) + EPSILON) * gain.reshape((1,) * (x.ndim - 1) + (-1,))


def silu(y):
    return y * (0.5 * jnp.tanh(0.5 * y) + 0.5)


def dot(a, b):
    return jnp.dot(a, b, preferred_element_type=F32)


def dot_t(a, b):
    return lax.dot_general(a, b, (((1,), (1,)), ((), ())), preferred_element_type=F32)


def pages_kernel(pages_ref, half_ref):
    half_ref[...] = pages_ref[1 - first_row()]


def first_row():
    return 1 - lax.rem(lax.axis_index("strip"), 2)


def lay_out(raw_ref, gain_ref, s, r, x_ref, act_ref, *index):
    frames, cols, width = raw_ref.shape[2:]
    to = lax.broadcasted_iota(jnp.int32, (cols * PAD, cols * frames), 0)
    at = lax.broadcasted_iota(jnp.int32, (cols * PAD, cols * frames), 1)
    pick = (at == lax.rem(to, PAD) * cols + to // PAD) & (lax.rem(to, PAD) < frames)
    rows = dot(pick.astype(F32).astype(BF16), raw_ref[s, r].reshape(frames * cols, width))
    for c in range(cols):
        ls = slice(c * width, (c + 1) * width)
        one = rows[c * PAD : (c + 1) * PAD]
        x_ref[(*index, slice(None), ls)] = one.astype(BF16)
        act_ref[(*index, slice(None), ls)] = silu(rms(one, gain_ref[...])).astype(BF16)


def edge_kernel(raw_ref, gain_ref, x_ref, act_ref):
    slots, rows = raw_ref.shape[:2]
    r = first_row() * (rows - 1)
    for s in range(slots):
        lay_out(raw_ref, gain_ref, s, r, x_ref, act_ref, s)


def act_kernel(raw_ref, gain_ref, edge_x_ref, edge_act_ref, x_ref, act_ref, edge_ref):
    slots, rows = raw_ref.shape[:2]
    done = first_row() * (rows - 1)
    other = rows - 1 - done
    x_ref[:, done] = edge_x_ref[...]
    act_ref[:, done] = edge_act_ref[...]
    for s in range(slots):
        for r in (other, *range(1, rows - 1)):
            lay_out(raw_ref, gain_ref, s, r, x_ref, act_ref, s, r)
        edge_ref[s] = act_ref[s, other]


def conv_kernel(x_ref, act_ref, near_ref, w_ref, bias_ref, out_ref, ext):
    slots, rows, _, wide = x_ref.shape
    width = wide // 2
    side = 2 * first_row()
    ext[:, 1 : rows + 1] = act_ref[...]
    ext[:, side // 2 * (rows + 1)] = near_ref[...]
    both = jnp.concatenate(
        [ext[:, 1 : rows + 1].reshape(-1, wide), ext[:, pl.ds(side, rows)].reshape(-1, wide)], axis=-1
    )
    inner = ext[:, pl.ds(2 - side // 2, rows - 1)].reshape(-1, wide)
    inner_rows = pl.ds(side // 2, rows - 1)
    weights = jnp.concatenate([pair_taps(w_ref, 1), pair_taps(w_ref, side)], axis=0)
    mid = dot(both, weights)
    rest = dot(inner, pair_taps(w_ref, 2 - side))
    for c in range(2):
        ls = slice(c * width, (c + 1) * width)
        out_ref[c] = (
            x_ref[:, :, :, ls].astype(F32) + bias_ref[...].reshape(1, 1, 1, width) + mid[:, ls].reshape(slots, rows, PAD, width)
        )
        out_ref[c, :, inner_rows] += rest[:, ls].reshape(slots, rows - 1, PAD, width)


def pair_taps(w_ref, dr):
    wide = 2 * w_ref.shape[2]
    return jnp.concatenate([w_ref[dr, 1 - c : 3 - c].reshape(wide, wide // 2) for c in range(2)], axis=1)


def apart(x):
    first = lax.broadcasted_iota(jnp.int32, x.shape, 1) < HEAD_DIM
    zero = jnp.zeros_like(x)
    return jnp.concatenate([jnp.where(first, x, zero), jnp.where(first, zero, x)], axis=0)


def time_kernel(
    frames, slot_ref, gate_ref, part_ref, next_ref, w_ref, tgain_ref, wq_ref, wk_ref, wv_ref, wo_ref,
    xgain_ref, xq_ref, after_ref, query_ref, choice_ref, live_ref, normed, tq, tk, tv, mixed, scores, chances,
    slot, gate, sems
):
    loads = [
        pltpu.make_async_copy(slot_ref, slot, sems.at[0]),
        pltpu.make_async_copy(gate_ref, gate, sems.at[1]),
    ]
    for load in loads:
        load.start()
    cols, slots, rows, _, width = part_ref.shape
    wide = 2 * width
    half = slots // 2
    total = cols * slots * rows * PAD
    side = 1 - first_row()
    strip = lax.axis_index("strip")

    @pl.when(jnp.where(side == 0, strip > 0, strip < lax.axis_size("strip") - 1))
    def _():
        add = dot(next_ref[...].reshape(-1, wide), pair_taps(w_ref, 2 * side))
        for c in range(2):
            part_ref[c, :, side * (rows - 1)] += add[:, c * width : (c + 1) * width].reshape(slots, PAD, width)

    normed[...] = rms(part_ref[...].reshape(total, width), tgain_ref[...]).astype(BF16)
    every = dot(normed[...], jnp.concatenate([wq_ref[...], wk_ref[...], wv_ref[...]], axis=1))
    for i, field in enumerate((tq, tk, tv)):
        field[...] = every[:, i * width : (i + 1) * width].astype(BF16)
    group = rows * PAD
    pair = 2 * HEAD_DIM
    row = lax.broadcasted_iota(jnp.int32, (group, 2 * group), 0)
    col = lax.rem(lax.broadcasted_iota(jnp.int32, (group, 2 * group), 1), group)
    mask = jnp.where((row // PAD == col // PAD) & (lax.rem(col, PAD) < frames), 0.0, NEG).astype(F32)
    first = lax.broadcasted_iota(jnp.int32, (group, 2 * group), 1) < group
    ones = apart(jnp.ones((group, pair), BF16))
    tiles = [
        (g, slice(g * group, (g + 1) * group), slice(j * pair, (j + 1) * pair))
        for g in range(total // group)
        for j in range(width // pair)
    ]
    for g, rs, ls in tiles:
        scores[rs, ls] = dot_t(tq[rs, ls], apart(tk[rs, ls]))
    for _, rs, ls in tiles:
        s = scores[rs, ls] + mask
        top = jnp.where(
            first,
            jnp.max(jnp.where(first, s, NEG), axis=-1, keepdims=True),
            jnp.max(jnp.where(first, NEG, s), axis=-1, keepdims=True),
        )
        chances[rs, ls] = jnp.exp2((s - top) * (0.125 * LOG2E)).astype(BF16)
    for _, rs, ls in tiles:
        out = dot(chances[rs, ls], jnp.concatenate([apart(tv[rs, ls]), ones], axis=1))
        mixed[rs, ls] = (out[:, :pair] / out[:, pair:]).astype(BF16)
    after_ref[...] = part_ref[...] + dot(mixed[...], wo_ref[...]).reshape(after_ref.shape)
    nc = rms(after_ref[:, :half], xgain_ref[...]).astype(BF16).reshape(-1, width)
    query_ref[...] = dot(nc, xq_ref[...]).astype(BF16).reshape(query_ref.shape)
    for load in loads:
        load.wait()
    first_page = lax.axis_index("req") * REQ_DEV
    for r in range(half):
        page = slot[first_page + r]
        i = lax.rem(page, REQ_DEV)
        place = i + jnp.where(page - i == first_page, 0, REQ_DEV)
        for j in range(2 * REQ_DEV):
            choice_ref[r, j] = jnp.full(choice_ref.shape[2:], jnp.where(place == j, 1.0, 0.0), F32).astype(BF16)
        live_ref[r] = jnp.full(live_ref.shape[1:], jnp.where(gate[r] == 1, 1.0, 0.0), F32)


def cross_kernel(
    frames, choice_ref, live_ref, after_ref, query_ref, own_ref, fetched_ref, swapped_ref, xo_ref, out_ref, keys, values, scores, chances, mixed, made, sems
):
    cols, slots, rows, _, width = after_ref.shape
    half = slots // 2
    even = first_row() == 1
    tokens = own_ref.shape[2]
    room = -(-tokens // 128) * 128
    group = cols * rows * PAD
    pair = 2 * HEAD_DIM
    for r in range(half):
        k = v = jnp.zeros((tokens, width), BF16)
        for i in range(REQ_DEV):
            mine, theirs = (choice_ref[r, j, 0:1] for j in (i, REQ_DEV + i))
            far_k = jnp.where(even, fetched_ref[i], swapped_ref[i])
            far_v = jnp.where(even, swapped_ref[i], fetched_ref[i])
            k += own_ref[0, i] * mine + far_k * theirs
            v += own_ref[1, i] * mine + far_v * theirs
        tail = jnp.zeros((room - tokens, width), BF16)
        keys[r] = jnp.concatenate([k, tail], axis=0)
        values[r] = jnp.concatenate([v, tail], axis=0)
    tiles = [(r, slice(j * pair, (j + 1) * pair), slice(2 * j * room, 2 * (j + 1) * room)) for r in range(half) for j in range(width // pair)]
    live = lax.rem(lax.broadcasted_iota(jnp.int32, (group, 2 * room), 1), room) < tokens
    ones = apart(jnp.ones((room, pair), BF16))
    for r, ls, ks in tiles:
        scores[r, :, ks] = dot_t(query_ref[:, r, :, :, ls].reshape(group, pair), apart(keys[r, :, ls]))
    for r, ls, ks in tiles:
        s = jnp.where(live, scores[r, :, ks], NEG)
        p = [jnp.exp2((t - jnp.max(t, axis=-1, keepdims=True)) * (0.125 * LOG2E)) for t in (s[:, :room], s[:, room:])]
        chances[r, :, ks] = jnp.concatenate(p, axis=1).astype(BF16)
    for r, ls, ks in tiles:
        out = dot(chances[r, :, ks], jnp.concatenate([apart(values[r, :, ls]), ones], axis=1))
        mixed[:, r, :, :, ls] = (out[:, :pair] / out[:, pair:]).astype(BF16).reshape(cols, rows, PAD, pair)
    frame = lax.broadcasted_iota(jnp.int32, (PAD, width), 0).astype(F32)
    scale = 1.0 + 2.0 * frame / (frames - 1)
    add = dot(mixed[...].reshape(-1, width), xo_ref[...]).reshape(cols, half, rows, PAD, width)
    copies = []
    for r in range(half):
        for w in range(rows):
            for c in range(cols):
                cond = (after_ref[c, r, w] + add[c, r, w]).astype(BF16).astype(F32)
                uncond = after_ref[c, half + r, w].astype(BF16).astype(F32)
                guided = jnp.where(live_ref[r] == 1.0, uncond + scale * (cond - uncond), cond)
                made[r, w, :, c, :] = guided[:frames].astype(BF16)
            copies.append(pltpu.make_async_copy(made.at[r, w], out_ref.at[r, w], sems.at[r, w]))
            copies[-1].start()
    for copy in copies:
        copy.wait()


def on_device(
    hidden_states, gate, context_slot, context_pages, conv_weight, conv_bias, conv_gain, temporal_gain,
    temporal_query, temporal_key, temporal_value, temporal_out, cross_gain, cross_query, cross_out,
):
    _, _, rows, cols, frames, width = hidden_states.shape
    slots = 2 * REQ_DEV
    count = lax.axis_size("req")
    partner_pairs = [(i, i ^ (count // 2)) for i in range(count)]
    strips = lax.axis_size("strip")
    near_pairs, next_pairs = (
        [p for i in range(start, strips - 1, 2) for p in ((i, i + 1), (i + 1, i))] for start in (0, 1)
    )

    vm = pl.BlockSpec(memory_space=pltpu.VMEM)
    any_ = pl.BlockSpec(memory_space=pl.ANY)
    total = cols * slots * rows * PAD
    wide = cols * width
    room = -(-context_pages.shape[2] // 128) * 128
    raw = hidden_states.reshape((slots, rows, cols, frames, width)).transpose(0, 1, 3, 2, 4)
    stored = context_pages.transpose(0, 2, 1, 3)
    half = pl.pallas_call(
        pages_kernel,
        out_shape=jax.ShapeDtypeStruct(stored.shape[1:], BF16),
        in_specs=[vm],
        out_specs=vm,
        compiler_params=pltpu.CompilerParams(vmem_limit_bytes=8 << 20),
        cost_estimate=cost(COSTP),
        name="pages",
    )(stored)
    keep = Layout(major_to_minor=(0, 1, 2))
    fetched = with_layout_constraint(lax.ppermute(half, "req", partner_pairs), keep)
    swapped = with_layout_constraint(lax.ppermute(fetched, "strip", near_pairs), keep)
    fetched = fetched.transpose(1, 0, 2)
    swapped = swapped.transpose(1, 0, 2)
    row = jax.ShapeDtypeStruct((slots, PAD, wide), BF16)
    whole = jax.ShapeDtypeStruct((slots, rows, PAD, wide), BF16)
    edge_x, edge_act = pl.pallas_call(
        edge_kernel,
        out_shape=(row, row),
        in_specs=[vm] * 2,
        out_specs=(vm, vm),
        compiler_params=pltpu.CompilerParams(vmem_limit_bytes=8 << 20),
        cost_estimate=cost(COST0),
        name="edge",
    )(raw, conv_gain)
    near = lax.ppermute(edge_act, "strip", near_pairs)
    x, act, edge = pl.pallas_call(
        act_kernel,
        out_shape=(whole, whole, row),
        in_specs=[vm] * 4,
        out_specs=(vm,) * 3,
        compiler_params=pltpu.CompilerParams(vmem_limit_bytes=8 << 20),
        cost_estimate=cost(COST1),
        name="activate",
    )(raw, conv_gain, edge_x, edge_act)
    other = lax.ppermute(edge, "strip", next_pairs)
    grid = (cols, slots, rows, PAD, width)
    part = pl.pallas_call(
        conv_kernel,
        out_shape=jax.ShapeDtypeStruct(grid, F32),
        in_specs=[vm] * 5,
        out_specs=vm,
        scratch_shapes=[pltpu.VMEM((slots, rows + 2, PAD, wide), BF16)],
        compiler_params=pltpu.CompilerParams(vmem_limit_bytes=16 << 20),
        cost_estimate=cost(COST1),
        name="conv_own",
    )(x, act, near, conv_weight, conv_bias)
    after, query, choice, live = pl.pallas_call(
        functools.partial(time_kernel, frames),
        out_shape=(
            jax.ShapeDtypeStruct(grid, F32),
            jax.ShapeDtypeStruct((cols, REQ_DEV, rows, PAD, width), BF16),
            jax.ShapeDtypeStruct((REQ_DEV, 2 * REQ_DEV, PAD, width), BF16),
            jax.ShapeDtypeStruct((REQ_DEV, PAD, width), F32),
        ),
        in_specs=[any_] * 2 + [vm] * 10,
        out_specs=(vm,) * 4,
        scratch_shapes=[pltpu.VMEM((total, width), BF16)] * 5
        + [pltpu.VMEM((total, width // HEAD_DIM * rows * PAD), kind) for kind in (F32, BF16)]
        + [pltpu.SMEM(context_slot.shape, jnp.int32), pltpu.SMEM(gate.shape, jnp.int32), pltpu.SemaphoreType.DMA((2,))],
        input_output_aliases={2: 0},
        compiler_params=pltpu.CompilerParams(vmem_limit_bytes=16 << 20),
        cost_estimate=cost(COST2),
        name="time_mix",
    )(
        context_slot, gate, part, other, conv_weight, temporal_gain, temporal_query, temporal_key, temporal_value,
        temporal_out, cross_gain, cross_query,
    )
    out = pl.pallas_call(
        functools.partial(cross_kernel, frames),
        out_shape=jax.ShapeDtypeStruct((REQ_DEV, rows, frames, cols, width), BF16),
        in_specs=[vm] * 8,
        out_specs=any_,
        scratch_shapes=[pltpu.VMEM((REQ_DEV, room, width), BF16)] * 2
        + [
            pltpu.VMEM((REQ_DEV, cols * rows * PAD, width // HEAD_DIM * room), F32),
            pltpu.VMEM((REQ_DEV, cols * rows * PAD, width // HEAD_DIM * room), BF16),
            pltpu.VMEM((cols, REQ_DEV, rows, PAD, width), BF16),
            pltpu.VMEM((REQ_DEV, rows, frames, cols, width), BF16),
            pltpu.SemaphoreType.DMA((REQ_DEV, rows)),
        ],
        compiler_params=pltpu.CompilerParams(vmem_limit_bytes=16 << 20),
        cost_estimate=cost(COST3),
        name="cross_mix",
    )(choice, live, after, query, context_pages, fetched, swapped, cross_out)
    return out.transpose(0, 1, 3, 2, 4)


def solution(mesh):
    return jax.shard_map(
        on_device,
        mesh=mesh,
        in_specs=(
            P(None, "req", "strip", None, None, None),
            P("req"),
            P(),
            P(None, "req", None, None),
        )
        + (P(),) * 11,
        out_specs=P("req", "strip", None, None, None),
        check_vma=False,
    )
```

```python
import functools
import jax
import jax.numpy as jnp
from jax import lax
from jax.experimental import pallas as pl
from jax.experimental.layout import Layout, with_layout_constraint
from jax.experimental.pallas import tpu as pltpu
from jax.sharding import PartitionSpec as P

HEAD_DIM = 64
REQ_DEV = 2
PAD = 16
EPSILON = 1e-06
LOG2E = 1.4426950408889634
F32 = jnp.float32
BF16 = jnp.bfloat16
NEG = -1e30
COSTP, COST0, COST1, COST2, COST3 = 3 * 10**9, 16 * 10**9, 3 * 10**8, 6 * 10**9, 10**9


def cost(flops):
    return pl.CostEstimate(flops=flops, bytes_accessed=0, transcendentals=0)


def rms(x, gain):
    return x * lax.rsqrt(jnp.mean(x * x, axis=-1, keepdims=True) + EPSILON) * gain.reshape((1,) * (x.ndim - 1) + (-1,))


def silu(y):
    return y * (0.5 * jnp.tanh(0.5 * y) + 0.5)


def dot(a, b):
    return jnp.dot(a, b, preferred_element_type=F32)


def dot_t(a, b):
    return lax.dot_general(a, b, (((1,), (1,)), ((), ())), preferred_element_type=F32)


def pages_kernel(pages_ref, half_ref):
    half_ref[...] = pages_ref[1 - first_row()]


def first_row():
    return 1 - lax.rem(lax.axis_index("strip"), 2)


def lay_out(raw_ref, gain_ref, s, r, x_ref, act_ref, *index):
    frames, cols, width = raw_ref.shape[2:]
    to = lax.broadcasted_iota(jnp.int32, (cols * PAD, cols * frames), 0)
    at = lax.broadcasted_iota(jnp.int32, (cols * PAD, cols * frames), 1)
    pick = (at == lax.rem(to, PAD) * cols + to // PAD) & (lax.rem(to, PAD) < frames)
    rows = dot(pick.astype(F32).astype(BF16), raw_ref[s, r].reshape(frames * cols, width))
    for c in range(cols):
        ls = slice(c * width, (c + 1) * width)
        one = rows[c * PAD : (c + 1) * PAD]
        x_ref[(*index, slice(None), ls)] = one.astype(BF16)
        act_ref[(*index, slice(None), ls)] = silu(rms(one, gain_ref[...])).astype(BF16)


def edge_kernel(raw_ref, gain_ref, x_ref, act_ref):
    slots, rows = raw_ref.shape[:2]
    r = first_row() * (rows - 1)
    for s in range(slots):
        lay_out(raw_ref, gain_ref, s, r, x_ref, act_ref, s)


def act_kernel(raw_ref, gain_ref, edge_x_ref, edge_act_ref, x_ref, act_ref, edge_ref):
    slots, rows = raw_ref.shape[:2]
    done = first_row() * (rows - 1)
    other = rows - 1 - done
    x_ref[:, done] = edge_x_ref[...]
    act_ref[:, done] = edge_act_ref[...]
    for s in range(slots):
        for r in (other, *range(1, rows - 1)):
            lay_out(raw_ref, gain_ref, s, r, x_ref, act_ref, s, r)
        edge_ref[s] = act_ref[s, other]


def conv_kernel(x_ref, act_ref, near_ref, w_ref, bias_ref, out_ref, ext):
    slots, rows, _, wide = x_ref.shape
    width = wide // 2
    side = 2 * first_row()
    ext[:, 1 : rows + 1] = act_ref[...]
    ext[:, side // 2 * (rows + 1)] = near_ref[...]
    both = jnp.concatenate(
        [ext[:, 1 : rows + 1].reshape(-1, wide), ext[:, pl.ds(side, rows)].reshape(-1, wide)], axis=-1
    )
    inner = ext[:, pl.ds(2 - side // 2, rows - 1)].reshape(-1, wide)
    inner_rows = pl.ds(side // 2, rows - 1)
    weights = jnp.concatenate([pair_taps(w_ref, 1), pair_taps(w_ref, side)], axis=0)
    mid = dot(both, weights)
    rest = dot(inner, pair_taps(w_ref, 2 - side))
    for c in range(2):
        ls = slice(c * width, (c + 1) * width)
        out_ref[c] = (
            x_ref[:, :, :, ls].astype(F32) + bias_ref[...].reshape(1, 1, 1, width) + mid[:, ls].reshape(slots, rows, PAD, width)
        )
        out_ref[c, :, inner_rows] += rest[:, ls].reshape(slots, rows - 1, PAD, width)


def pair_taps(w_ref, dr):
    wide = 2 * w_ref.shape[2]
    return jnp.concatenate([w_ref[dr, 1 - c : 3 - c].reshape(wide, wide // 2) for c in range(2)], axis=1)


def apart(x):
    first = lax.broadcasted_iota(jnp.int32, x.shape, 1) < HEAD_DIM
    zero = jnp.zeros_like(x)
    return jnp.concatenate([jnp.where(first, x, zero), jnp.where(first, zero, x)], axis=0)


def time_kernel(
    frames, slot_ref, gate_ref, part_ref, next_ref, w_ref, tgain_ref, wq_ref, wk_ref, wv_ref, wo_ref,
    xgain_ref, xq_ref, _part, after_ref, query_ref, choice_ref, live_ref, normed, tq, tk, tv, mixed, scores, chances,
    slot, gate, sems
):
    loads = [
        pltpu.make_async_copy(slot_ref, slot, sems.at[0]),
        pltpu.make_async_copy(gate_ref, gate, sems.at[1]),
    ]
    for load in loads:
        load.start()
    cols, slots, rows, _, width = part_ref.shape
    wide = 2 * width
    half = slots // 2
    total = cols * slots * rows * PAD
    side = 1 - first_row()
    strip = lax.axis_index("strip")

    @pl.when(jnp.where(side == 0, strip > 0, strip < lax.axis_size("strip") - 1))
    def _():
        add = dot(next_ref[...].reshape(-1, wide), pair_taps(w_ref, 2 * side))
        for c in range(2):
            part_ref[c, :, side * (rows - 1)] += add[:, c * width : (c + 1) * width].reshape(slots, PAD, width)

    normed[...] = rms(part_ref[...].reshape(total, width), tgain_ref[...]).astype(BF16)
    every = dot(normed[...], jnp.concatenate([wq_ref[...], wk_ref[...], wv_ref[...]], axis=1))
    for i, field in enumerate((tq, tk, tv)):
        field[...] = every[:, i * width : (i + 1) * width].astype(BF16)
    group = rows * PAD
    pair = 2 * HEAD_DIM
    row = lax.broadcasted_iota(jnp.int32, (group, 2 * group), 0)
    col = lax.rem(lax.broadcasted_iota(jnp.int32, (group, 2 * group), 1), group)
    mask = jnp.where((row // PAD == col // PAD) & (lax.rem(col, PAD) < frames), 0.0, NEG).astype(F32)
    first = lax.broadcasted_iota(jnp.int32, (group, 2 * group), 1) < group
    ones = apart(jnp.ones((group, pair), BF16))
    tiles = [
        (g, slice(g * group, (g + 1) * group), slice(j * pair, (j + 1) * pair))
        for g in range(total // group)
        for j in range(width // pair)
    ]
    for g, rs, ls in tiles:
        scores[rs, ls] = dot_t(tq[rs, ls], apart(tk[rs, ls]))
    for _, rs, ls in tiles:
        s = scores[rs, ls] + mask
        top = jnp.where(
            first,
            jnp.max(jnp.where(first, s, NEG), axis=-1, keepdims=True),
            jnp.max(jnp.where(first, NEG, s), axis=-1, keepdims=True),
        )
        chances[rs, ls] = jnp.exp2((s - top) * (0.125 * LOG2E)).astype(BF16)
    for _, rs, ls in tiles:
        out = dot(chances[rs, ls], jnp.concatenate([apart(tv[rs, ls]), ones], axis=1))
        mixed[rs, ls] = (out[:, :pair] / out[:, pair:]).astype(BF16)
    add = dot(mixed[...], wo_ref[...]).reshape(part_ref.shape)
    cond = part_ref[:, :half] + add[:, :half]
    nc = rms(cond, xgain_ref[...]).astype(BF16).reshape(-1, width)
    query_ref[...] = dot(nc, xq_ref[...]).astype(BF16).reshape(query_ref.shape)
    for load in loads:
        load.wait()
    first_page = lax.axis_index("req") * REQ_DEV
    for r in range(half):
        page = slot[first_page + r]
        i = lax.rem(page, REQ_DEV)
        place = i + jnp.where(page - i == first_page, 0, REQ_DEV)
        for j in range(2 * REQ_DEV):
            choice_ref[r, j] = jnp.full(choice_ref.shape[2:], jnp.where(place == j, 1.0, 0.0), F32).astype(BF16)
        frame = lax.broadcasted_iota(jnp.int32, (PAD, width), 0).astype(F32)
        guide = 1.0 + 2.0 * frame / (frames - 1)
        live_ref[r] = jnp.where(gate[r] == 1, guide, 1.0)
        for c in range(2):
            uncond = part_ref[c, half + r] + add[c, half + r]
            after_ref[c, r] = jnp.where(gate[r] == 1, uncond + guide * (cond[c, r] - uncond), cond[c, r])


def cross_kernel(
    frames, choice_ref, live_ref, after_ref, query_ref, own_ref, fetched_ref, swapped_ref, xo_ref, out_ref, keys, values, scores, chances, mixed, made, sems
):
    cols, half, rows, _, width = after_ref.shape
    even = first_row() == 1
    tokens = own_ref.shape[2]
    room = -(-tokens // 128) * 128
    group = cols * rows * PAD
    pair = 2 * HEAD_DIM
    for r in range(half):
        k = v = jnp.zeros((tokens, width), BF16)
        for i in range(REQ_DEV):
            mine, theirs = (choice_ref[r, j, 0:1] for j in (i, REQ_DEV + i))
            far_k = jnp.where(even, fetched_ref[i], swapped_ref[i])
            far_v = jnp.where(even, swapped_ref[i], fetched_ref[i])
            k += own_ref[0, i] * mine + far_k * theirs
            v += own_ref[1, i] * mine + far_v * theirs
        tail = jnp.zeros((room - tokens, width), BF16)
        keys[r] = jnp.concatenate([k, tail], axis=0)
        values[r] = jnp.concatenate([v, tail], axis=0)
    tiles = [(r, slice(j * pair, (j + 1) * pair), slice(2 * j * room, 2 * (j + 1) * room)) for r in range(half) for j in range(width // pair)]
    live = lax.rem(lax.broadcasted_iota(jnp.int32, (group, 2 * room), 1), room) < tokens
    ones = apart(jnp.ones((room, pair), BF16))
    for r, ls, ks in tiles:
        scores[r, :, ks] = dot_t(query_ref[:, r, :, :, ls].reshape(group, pair), apart(keys[r, :, ls]))
    for r, ls, ks in tiles:
        s = jnp.where(live, scores[r, :, ks], NEG)
        p = [jnp.exp2((t - jnp.max(t, axis=-1, keepdims=True)) * (0.125 * LOG2E)) for t in (s[:, :room], s[:, room:])]
        chances[r, :, ks] = jnp.concatenate(p, axis=1).astype(BF16)
    for r, ls, ks in tiles:
        out = dot(chances[r, :, ks], jnp.concatenate([apart(values[r, :, ls]), ones], axis=1))
        mixed[:, r, :, :, ls] = (out[:, :pair] / out[:, pair:]).astype(BF16).reshape(cols, rows, PAD, pair)
    add = dot(mixed[...].reshape(-1, width), xo_ref[...]).reshape(cols, half, rows, PAD, width)
    copies = []
    for r in range(half):
        for w in range(rows):
            for c in range(cols):
                guided = after_ref[c, r, w] + live_ref[r] * add[c, r, w]
                made[r, w, :, c, :] = guided[:frames].astype(BF16)
            copies.append(pltpu.make_async_copy(made.at[r, w], out_ref.at[r, w], sems.at[r, w]))
            copies[-1].start()
    for copy in copies:
        copy.wait()


def on_device(
    hidden_states, gate, context_slot, context_pages, conv_weight, conv_bias, conv_gain, temporal_gain,
    temporal_query, temporal_key, temporal_value, temporal_out, cross_gain, cross_query, cross_out,
):
    _, _, rows, cols, frames, width = hidden_states.shape
    slots = 2 * REQ_DEV
    count = lax.axis_size("req")
    partner_pairs = [(i, i ^ (count // 2)) for i in range(count)]
    strips = lax.axis_size("strip")
    near_pairs, next_pairs = (
        [p for i in range(start, strips - 1, 2) for p in ((i, i + 1), (i + 1, i))] for start in (0, 1)
    )

    vm = pl.BlockSpec(memory_space=pltpu.VMEM)
    any_ = pl.BlockSpec(memory_space=pl.ANY)
    total = cols * slots * rows * PAD
    wide = cols * width
    room = -(-context_pages.shape[2] // 128) * 128
    raw = hidden_states.reshape((slots, rows, cols, frames, width)).transpose(0, 1, 3, 2, 4)
    stored = context_pages.transpose(0, 2, 1, 3)
    half = pl.pallas_call(
        pages_kernel,
        out_shape=jax.ShapeDtypeStruct(stored.shape[1:], BF16),
        in_specs=[vm],
        out_specs=vm,
        compiler_params=pltpu.CompilerParams(vmem_limit_bytes=8 << 20),
        cost_estimate=cost(COSTP),
        name="pages",
    )(stored)
    keep = Layout(major_to_minor=(0, 1, 2))
    fetched = with_layout_constraint(lax.ppermute(half, "req", partner_pairs), keep)
    swapped = with_layout_constraint(lax.ppermute(fetched, "strip", near_pairs), keep)
    fetched = fetched.transpose(1, 0, 2)
    swapped = swapped.transpose(1, 0, 2)
    row = jax.ShapeDtypeStruct((slots, PAD, wide), BF16)
    whole = jax.ShapeDtypeStruct((slots, rows, PAD, wide), BF16)
    edge_x, edge_act = pl.pallas_call(
        edge_kernel,
        out_shape=(row, row),
        in_specs=[vm] * 2,
        out_specs=(vm, vm),
        compiler_params=pltpu.CompilerParams(vmem_limit_bytes=8 << 20),
        cost_estimate=cost(COST0),
        name="edge",
    )(raw, conv_gain)
    near = lax.ppermute(edge_act, "strip", near_pairs)
    x, act, edge = pl.pallas_call(
        act_kernel,
        out_shape=(whole, whole, row),
        in_specs=[vm] * 4,
        out_specs=(vm,) * 3,
        compiler_params=pltpu.CompilerParams(vmem_limit_bytes=8 << 20),
        cost_estimate=cost(COST1),
        name="activate",
    )(raw, conv_gain, edge_x, edge_act)
    other = lax.ppermute(edge, "strip", next_pairs)
    grid = (cols, slots, rows, PAD, width)
    part = pl.pallas_call(
        conv_kernel,
        out_shape=jax.ShapeDtypeStruct(grid, F32),
        in_specs=[vm] * 5,
        out_specs=vm,
        scratch_shapes=[pltpu.VMEM((slots, rows + 2, PAD, wide), BF16)],
        compiler_params=pltpu.CompilerParams(vmem_limit_bytes=16 << 20),
        cost_estimate=cost(COST1),
        name="conv_own",
    )(x, act, near, conv_weight, conv_bias)
    _, after, query, choice, live = pl.pallas_call(
        functools.partial(time_kernel, frames),
        out_shape=(
            jax.ShapeDtypeStruct(grid, F32),
            jax.ShapeDtypeStruct((cols, REQ_DEV, rows, PAD, width), F32),
            jax.ShapeDtypeStruct((cols, REQ_DEV, rows, PAD, width), BF16),
            jax.ShapeDtypeStruct((REQ_DEV, 2 * REQ_DEV, PAD, width), BF16),
            jax.ShapeDtypeStruct((REQ_DEV, PAD, width), F32),
        ),
        in_specs=[any_] * 2 + [vm] * 10,
        out_specs=(vm,) * 5,
        scratch_shapes=[pltpu.VMEM((total, width), BF16)] * 5
        + [pltpu.VMEM((total, width // HEAD_DIM * rows * PAD), kind) for kind in (F32, BF16)]
        + [pltpu.SMEM(context_slot.shape, jnp.int32), pltpu.SMEM(gate.shape, jnp.int32), pltpu.SemaphoreType.DMA((2,))],
        input_output_aliases={2: 0},
        compiler_params=pltpu.CompilerParams(vmem_limit_bytes=16 << 20),
        cost_estimate=cost(COST2),
        name="time_mix",
    )(
        context_slot, gate, part, other, conv_weight, temporal_gain, temporal_query, temporal_key, temporal_value,
        temporal_out, cross_gain, cross_query,
    )
    out = pl.pallas_call(
        functools.partial(cross_kernel, frames),
        out_shape=jax.ShapeDtypeStruct((REQ_DEV, rows, frames, cols, width), BF16),
        in_specs=[vm] * 8,
        out_specs=any_,
        scratch_shapes=[pltpu.VMEM((REQ_DEV, room, width), BF16)] * 2
        + [
            pltpu.VMEM((REQ_DEV, cols * rows * PAD, width // HEAD_DIM * room), F32),
            pltpu.VMEM((REQ_DEV, cols * rows * PAD, width // HEAD_DIM * room), BF16),
            pltpu.VMEM((cols, REQ_DEV, rows, PAD, width), BF16),
            pltpu.VMEM((REQ_DEV, rows, frames, cols, width), BF16),
            pltpu.SemaphoreType.DMA((REQ_DEV, rows)),
        ],
        compiler_params=pltpu.CompilerParams(vmem_limit_bytes=16 << 20),
        cost_estimate=cost(COST3),
        name="cross_mix",
    )(choice, live, after, query, context_pages, fetched, swapped, cross_out)
    return out.transpose(0, 1, 3, 2, 4)


def solution(mesh):
    return jax.shard_map(
        on_device,
        mesh=mesh,
        in_specs=(
            P(None, "req", "strip", None, None, None),
            P("req"),
            P(),
            P(None, "req", None, None),
        )
        + (P(),) * 11,
        out_specs=P("req", "strip", None, None, None),
        check_vma=False,
    )
```
